512 devices in a mesh: grp: 4 (over x), head: 16 (over z, core), sub: 8 (over y).
Axes of the slice: x: 4, y: 8, z: 8, core: 2. Of those that a mesh axis runs over, the one named last changes fastest.
Arguments:
- inputs: bfloat16 [512, 2048], P('grp', 'sub'), may hold values from -6 to 6
- in_gain: float32 [2048], P('sub'), may hold values from 0.5 to 1.5
- w_qkvz: bfloat16 [2048, 8192], P('sub', 'head'), may hold values from -0.125 to 0.125
- w_ab: bfloat16 [2048, 32], P('sub', 'head'), may hold values from -0.125 to 0.125
- a_log: float32 [16], P('head'), may hold values from -1.5 to 1.5
- dt_bias: float32 [16], P('head'), may hold values from -2 to 1
- state_values: bfloat16 [512, 16, 128, 128], P(('grp', 'sub'), 'head'), may hold values from -1 to 1
- state_scales: float32 [512, 16, 128], P(('grp', 'sub'), 'head'), may hold values from 0.05 to 0.5
- norm_gain: float32 [128], replicated, may hold values from 0.5 to 1.5
- w_out: bfloat16 [2048, 2048], P('head', 'sub'), may hold values from -0.125 to 0.125
- post_gain: float32 [2048], replicated, may hold values from 0.5 to 1.5
- routes: int32 [512, 10], P(('grp', 'head')), may hold values from 0 to 255, all different within a row; in each aligned block of 8 rows (0 to 7, 8 to 15, ...) at most 2 rows name the same one
- route_scale: int32 [512, 10], P(('grp', 'head')), may hold values from 8 to 32
- w_gate_up: bfloat16 [512, 2048, 512], P(('grp', 'head', 'sub')), may hold values from -0.125 to 0.125
- w_down: bfloat16 [512, 256, 2048], P(('grp', 'head', 'sub')), may hold values from -0.25 to 0.25
Outputs:
- out: bfloat16 [512, 2048], P(('grp', 'head'), 'sub')
- new_values: bfloat16 [512, 16, 128, 128], P(('grp', 'sub'), 'head')
- new_scales: float32 [512, 16, 128], P(('grp', 'sub'), 'head')
The draws below stay inside these ranges and needn't reach their ends.
Inputs may be any that keep to these rules, and one draw needn't show every extreme that they name: `routes`: each row names 10 different experts; within each aligned block of 8 rows no expert is named by more than 2 rows.
All inputs are finite; a program needn't handle non-finite values. Where the reference program divides by a largest or mean magnitude, that divisor is 1e-20 or more.
Results may differ from the reference program's by a relative error of at most 0.03.
Values may be sent and summed in bfloat16 or wider, within the bound.
No kernel may reach another device: no remote copies, remote signals or barrier semaphores. Data moves between devices by JAX's collectives and lax.ppermute only.
A program may use at most 64 MiB of HBM per device.

```python
import math
import jax
import jax.numpy as jnp
import numpy as np
from jax import lax

D = 2048
HEAD_DIM = 128
MOE_FF = 512
TOPK = 10
FF_HALF = 256
VHEADS = 16
EXPERTS = 256
BLOCK = 8
MOST = 2
ROWS = 512


def plant(result, rng, smallest, top_value):
    shape = result.shape
    place = [jax.random.randint(jax.random.fold_in(rng, axis), (), 0, shape[axis]) for axis in range(len(shape))]
    result = result.at[tuple(place)].set(smallest)
    longest = shape.index(max(shape))
    place[longest] = (place[longest] + 1) % shape[longest]
    return result.at[tuple(place)].set(top_value)


def shard_levels(stream_key, extent, split, low, high):
    level = 1.0
    for axis_at, blocks in split:
        heights = jax.random.uniform(jax.random.fold_in(jax.random.fold_in(stream_key, 6), axis_at), (blocks,), jnp.float32, low / len(split), high / len(split))
        level = level * jnp.repeat(jnp.exp(heights), extent[axis_at] // blocks).reshape((-1,) + (1,) * (len(extent) - 1 - axis_at))
    return level


def shared_out(key, own, number, rows, amount, top, most, lean):
    ranking = jax.random.permutation(key, amount)
    heavy_load, usual = load_shares(amount, rows * top, most, lean, True), load_shares(amount, rows * top, most, lean, False)
    places = jnp.arange(amount)

    def named(lengths, offset_by):
        used = int((lengths > 0).sum())
        fixed = max(1, used // 4)
        moved = fixed + (places - fixed + offset_by * (used - fixed)) % max(1, amount - fixed)
        return jnp.zeros((amount,), jnp.int32).at[ranking[jnp.where(places < fixed, places, moved)]].set(jnp.asarray(lengths, jnp.int32))

    lengths = jnp.where(number % 4 == 0, named(heavy_load, number // 4), named(usual, number - number // 4 - 1))
    mixed = jax.random.permutation(jax.random.fold_in(own, 3), amount)
    source_of, receiver = mixed[0:amount // 2 * 2:2], mixed[1:amount // 2 * 2:2]
    room = jnp.minimum(lengths[source_of] - 1, most - lengths[receiver]) // 2
    room = jnp.where((source_of == ranking[0]) | (receiver == ranking[0]) | (lengths[receiver] == 0), 0, jnp.maximum(room, 0))
    moved = jax.random.randint(jax.random.fold_in(own, 4), (amount // 2,), 0, 1 << 20) % (room + 1)
    lengths = lengths.at[source_of].add(-moved).at[receiver].add(moved)
    items = jnp.searchsorted(jnp.cumsum(lengths), jnp.arange(rows * top), side="right").astype(jnp.int32)
    grid = items.reshape(top, rows).T
    grid = grid[jax.random.permutation(jax.random.fold_in(own, 1), rows)]
    offset_by = jax.random.randint(jax.random.fold_in(own, 2), (rows, 1), 0, top)
    return jnp.take_along_axis(grid, (jnp.arange(top)[None, :] + offset_by) % top, axis=1)


def load_shares(count, total, reach, lean, full):
    portions = [(1 << 20) // math.isqrt(rank ** lean) + 1 for rank in range(1, count + 1)]
    largest = reach if full else min(reach, max(-(-total // count), total * portions[0] // sum(portions)))
    least = 1 if total - largest >= count - 1 else 0
    counts, rest = [largest] + [least] * (count - 1), total - largest - least * (count - 1)
    while rest > 0:
        movable = [i for i in range(1, count) if counts[i] < largest] or [i for i in range(1, count) if counts[i] < reach]
        whole, left = sum([portions[i] for i in movable]), rest
        for i in movable:
            addition = min(reach - counts[i], max(1, left * portions[i] // whole), rest)
            counts[i] = counts[i] + addition
            rest = rest - addition
    return np.array(counts)


def scatter_about(stream_key, shape, scale, limit, split=(), kind=jnp.bfloat16):
    drawn = jax.random.normal(stream_key, shape, jnp.float32) * scale
    if len(split) > 0:
        drawn = shard_levels(stream_key, shape, split, -0.22, 0.18) * drawn
    return jnp.clip(drawn, min=-limit, max=limit).astype(kind)


def setup_inputs(seed: int = 0) -> dict:
    key_of = jax.random.split(jax.random.key(seed), 16)
    inputs = scatter_about(key_of[0], (ROWS, D), 1.0, 6.0, ((0, 4), (1, 8)))
    in_gain = jnp.clip(1.0 + 0.1 * jax.random.normal(key_of[1], (D,), jnp.float32), 0.5, 1.5)
    w_qkvz = scatter_about(key_of[2], (D, VHEADS * 4 * HEAD_DIM), D ** -0.5, 0.125, ((0, 8), (1, 16)))
    w_ab = scatter_about(key_of[3], (D, 2 * VHEADS), D ** -0.5, 0.125, ((0, 8), (1, 16)))
    a_log = jnp.clip(jax.random.uniform(key_of[4], (VHEADS,), jnp.float32, -1.5, 1.5) * shard_levels(key_of[4], (VHEADS,), ((0, 16),), -0.4, 0.0), -1.5, 1.5)
    dt_bias = jnp.clip(-2.0 + 3.0 * jax.random.uniform(key_of[5], (VHEADS,), jnp.float32) ** shard_levels(key_of[5], (VHEADS,), ((0, 16),), -0.2, 0.2), -2.0, 1.0)
    state_values = jnp.clip(jax.random.uniform(key_of[6], (ROWS, VHEADS, HEAD_DIM, HEAD_DIM), jnp.float32, -1.0, 1.0) * shard_levels(key_of[6], (ROWS, VHEADS, HEAD_DIM, HEAD_DIM), ((0, 32), (1, 16)), -0.4, 0.0), -1.0, 1.0).astype(jnp.bfloat16)
    state_scales = jnp.clip(jnp.exp(math.log(0.5) - 2.3025851 * jax.random.uniform(key_of[7], (ROWS, VHEADS, HEAD_DIM), jnp.float32) ** shard_levels(key_of[7], (ROWS, VHEADS, HEAD_DIM), ((0, 32), (1, 16)), -0.2, 0.2)), 0.05, 0.5)
    norm_gain = jnp.clip(1.0 + 0.1 * jax.random.normal(key_of[8], (HEAD_DIM,), jnp.float32), 0.5, 1.5)
    w_out = scatter_about(key_of[9], (VHEADS * HEAD_DIM, D), (VHEADS * HEAD_DIM) ** -0.5, 0.125, ((0, 16), (1, 8)))
    post_gain = jnp.clip(1.0 + 0.1 * jax.random.normal(key_of[10], (D,), jnp.float32), 0.5, 1.5)
    routes_keys = jax.random.split(jax.random.fold_in(key_of[11], 1), ROWS // BLOCK)
    routes_turns = jax.random.permutation(jax.random.fold_in(key_of[11], 3), ROWS // BLOCK)
    routes = jax.vmap(lambda own, number: shared_out(jax.random.fold_in(key_of[11], 2), own, number, BLOCK, EXPERTS, TOPK, MOST, 2))(routes_keys, routes_turns).reshape((ROWS, TOPK))
    route_scale = plant(jax.random.randint(key_of[12], (ROWS, TOPK), 8, 33), jax.random.fold_in(key_of[12], 1), 8, 32).astype(jnp.int32)
    w_gate_up = scatter_about(key_of[13], (2 * EXPERTS, D, 2 * FF_HALF), D ** -0.5, 0.125, ((0, 512),))
    w_down = scatter_about(key_of[14], (2 * EXPERTS, FF_HALF, D), MOE_FF ** -0.5, 0.25, ((0, 512),))
    return dict(inputs=inputs, in_gain=in_gain, w_qkvz=w_qkvz, w_ab=w_ab, a_log=a_log, dt_bias=dt_bias, state_values=state_values, state_scales=state_scales, norm_gain=norm_gain, w_out=w_out, post_gain=post_gain, routes=routes, route_scale=route_scale, w_gate_up=w_gate_up, w_down=w_down)


def reference(inputs, in_gain, w_qkvz, w_ab, a_log, dt_bias, state_values, state_scales, norm_gain, w_out, post_gain, routes, route_scale, w_gate_up, w_down):
    highest_precision = lax.Precision.HIGHEST
    xf = inputs.astype(jnp.float32)
    ms_in = lax.optimization_barrier(jnp.mean(xf * xf, axis=1))
    xg = (xf * in_gain).astype(jnp.bfloat16)
    scale = lax.rsqrt(ms_in + 1e-05)[:, None]
    proj = jnp.dot(xg, w_qkvz, preferred_element_type=jnp.float32) * scale
    gates = jnp.dot(xg, w_ab, preferred_element_type=jnp.float32) * scale
    proj = proj.reshape(ROWS, VHEADS, 4, HEAD_DIM)
    gates = gates.reshape(ROWS, VHEADS, 2)
    query = jax.nn.silu(proj[:, :, 0])
    keys = jax.nn.silu(proj[:, :, 1])
    value = jax.nn.silu(proj[:, :, 2])
    zgate = proj[:, :, 3]
    query = query * lax.rsqrt(lax.optimization_barrier(jnp.sum(query * query, axis=-1, keepdims=True)) + 1e-06) / jnp.sqrt(jnp.float32(HEAD_DIM))
    keys = keys * lax.rsqrt(lax.optimization_barrier(jnp.sum(keys * keys, axis=-1, keepdims=True)) + 1e-06)
    beta = jax.nn.sigmoid(gates[:, :, 1])
    decay = jnp.exp(-jnp.exp(a_log)[None, :] * jax.nn.softplus(gates[:, :, 0] + dt_bias[None, :]))
    state = state_values.astype(jnp.float32) * state_scales[..., None]
    state = state * decay[:, :, None, None]
    memory = jnp.einsum('rhkv,rhk->rhv', state, keys, precision=highest_precision)
    delta = (value - memory) * beta[..., None]
    state = state + keys[..., :, None] * delta[..., None, :]
    core = jnp.einsum('rhkv,rhk->rhv', state, query, precision=highest_precision)
    gated = core * lax.rsqrt(lax.optimization_barrier(jnp.mean(core * core, axis=-1, keepdims=True)) + 1e-06) * norm_gain * jax.nn.silu(zgate)
    gated = gated.astype(jnp.bfloat16).reshape(ROWS, VHEADS * HEAD_DIM)
    peak = lax.optimization_barrier(jnp.max(jnp.abs(state), axis=-1)) + 1e-06
    new_values = (state / peak[..., None]).astype(jnp.bfloat16)
    attn = jnp.dot(gated, w_out, preferred_element_type=jnp.float32)
    hidden = (xf + attn).astype(jnp.bfloat16)
    hf = hidden.astype(jnp.float32)
    normed = (hf * lax.rsqrt(lax.optimization_barrier(jnp.mean(hf * hf, axis=1, keepdims=True)) + 1e-05) * post_gain).astype(jnp.bfloat16)

    def one_row(item):
        token_row, picks, numer = item
        halves = jnp.stack([2 * picks, 2 * picks + 1], axis=1).astype(jnp.int32)
        up_weight_stack = w_gate_up[halves].astype(jnp.float32)
        down_weight_stack = w_down[halves].astype(jnp.float32)
        gate_up_joint = jnp.einsum('r,uiry->uiy', token_row.astype(jnp.float32), up_weight_stack, precision=highest_precision)
        activated_hidden = (jax.nn.silu(gate_up_joint[..., :FF_HALF]) * gate_up_joint[..., FF_HALF:]).astype(jnp.bfloat16)
        half_output_width = jnp.einsum('tsu,tsug->tsg', activated_hidden.astype(jnp.float32), down_weight_stack, precision=highest_precision).astype(jnp.bfloat16)
        weights = numer.astype(jnp.float32) / 32.0
        return lax.optimization_barrier(jnp.sum(weights[:, None, None] * half_output_width.astype(jnp.float32), axis=(0, 1)))
    moe = lax.map(one_row, (normed, routes, route_scale))
    out = (hf + moe).astype(jnp.bfloat16)
    return (out, new_values, peak)
```

```python
import jax
import jax.numpy as jnp
from jax import lax
from jax.experimental import pallas as pl
from jax.experimental.pallas import tpu as pltpu
from jax.sharding import PartitionSpec as P

D = 2048
HD = 128
TOPK = 10
F32 = jnp.float32
BF16 = jnp.bfloat16

VM = pl.BlockSpec(memory_space=pltpu.VMEM)
SM = pl.BlockSpec(memory_space=pltpu.SMEM)


def call(body, outs, ins, operands, scratch=(), vmem=32 << 20):
    return pl.pallas_call(
        body,
        out_shape=outs,
        in_specs=ins,
        out_specs=jax.tree.map(lambda _: VM, outs),
        scratch_shapes=list(scratch),
        compiler_params=pltpu.CompilerParams(vmem_limit_bytes=vmem),
    )(*operands)


def split_hi(x):
    hi = x.astype(BF16).astype(F32)
    return hi, x - hi


def project_body(x_ref, gain_ref, w_ref, wab_ref, out_ref):
    xf = x_ref[...].astype(F32)
    xg = (xf * gain_ref[...]).astype(BF16)
    proj = jnp.dot(xg, w_ref[...], preferred_element_type=F32)
    key_hi, key_lo = split_hi(proj[:, 128:256])
    out_ref[:, :128] = proj[:, :128].astype(BF16)
    out_ref[:, 128:256] = key_hi.astype(BF16)
    out_ref[:, 256:512] = proj[:, 256:].astype(BF16)
    out_ref[:, 512:640] = key_lo.astype(BF16)
    xgf = xg.astype(F32)
    a = jnp.sum(xgf * wab_ref[0:1, :].astype(F32), axis=1, keepdims=True)
    b = jnp.sum(xgf * wab_ref[1:2, :].astype(F32), axis=1, keepdims=True)
    s = jnp.sum(xf * xf, axis=1, keepdims=True)
    lane = lax.broadcasted_iota(jnp.int32, (xf.shape[0], 128), 1)
    tail = jnp.zeros((xf.shape[0], 128), F32)
    at = 0
    for v in (a, b, s):
        hi, lo = split_hi(v)
        tail = jnp.where(lane == at, hi, tail)
        tail = jnp.where(lane == at + 1, lo, tail)
        at += 2
    out_ref[:, 640:] = tail.astype(BF16)


def silu(x):
    return x * jax.nn.sigmoid(x)


def recur_body(
    p_ref, alog_ref, bias_ref, sv_ref, ss_ref, gain_ref, gated_ref, keys_ref, delta_ref, sd_ref
):
    rows = 16
    t = p_ref[0:rows, :].astype(F32)
    for i in range(1, 8):
        t = t + p_ref[i * rows : (i + 1) * rows, :].astype(F32)
    tail = t[:, 640:]
    lane = lax.broadcasted_iota(jnp.int32, (rows, 128), 1)

    def column(i):
        return jnp.sum(
            jnp.where((lane == i) | (lane == i + 1), tail, 0.0), axis=1, keepdims=True
        )

    scale = lax.rsqrt(column(4) / D + 1e-05)
    proj = t[:, :512] * scale
    av = column(0) * scale
    bv = column(2) * scale
    query = silu(proj[:, :128])
    keys = silu(proj[:, 128:256] + t[:, 512:640] * scale)
    value = silu(proj[:, 256:384])
    zgate = proj[:, 384:512]
    query = (
        query
        * lax.rsqrt(jnp.sum(query * query, axis=-1, keepdims=True) + 1e-06)
        * (1.0 / 128.0**0.5)
    )
    keys = keys * lax.rsqrt(jnp.sum(keys * keys, axis=-1, keepdims=True) + 1e-06)
    beta = jax.nn.sigmoid(bv)
    rate = jnp.exp(jnp.zeros((1, 1), F32) + alog_ref[0])
    pre = av + bias_ref[0]
    soft = jnp.maximum(pre, 0.0) + jnp.log(1.0 + jnp.exp(-jnp.abs(pre)))
    decay = jnp.exp(-rate * soft)
    sd = ss_ref[...] * decay
    kd = (keys * sd).T
    qd = (query * sd).T
    mems = []
    cores = []
    for r in range(rows):
        v = sv_ref[r].astype(F32)
        mems.append(jnp.sum(v * kd[:, r : r + 1], axis=0, keepdims=True))
        cores.append(jnp.sum(v * qd[:, r : r + 1], axis=0, keepdims=True))
    memory = jnp.concatenate(mems, axis=0)
    core0 = jnp.concatenate(cores, axis=0)
    delta = (value - memory) * beta
    core = core0 + jnp.sum(query * keys, axis=-1, keepdims=True) * delta
    gated = (
        core
        * lax.rsqrt(jnp.mean(core * core, axis=-1, keepdims=True) + 1e-06)
        * gain_ref[...]
        * silu(zgate)
    )
    gated_ref[...] = gated.astype(BF16)
    keys_ref[...] = keys
    delta_ref[...] = delta
    sd_ref[...] = sd


def state_body(sv_ref, sd_ref, keys_ref, delta_ref, nv_ref, ns_ref):
    rows = 16
    sdt = sd_ref[...].T
    kt = keys_ref[...].T
    lane = lax.broadcasted_iota(jnp.int32, (128, rows), 1)
    peaks = jnp.zeros((128, rows), F32)
    for r in range(rows):
        s = sv_ref[r].astype(F32) * sdt[:, r : r + 1] + kt[:, r : r + 1] * delta_ref[r : r + 1, :]
        peak = jnp.max(jnp.abs(s), axis=1, keepdims=True) + 1e-06
        nv_ref[r] = (s / peak).astype(BF16)
        peaks = jnp.where(lane == r, peak, peaks)
    ns_ref[...] = peaks.T


def route_body(pair_ref, routes_ref, scale_ref, mt_ref, w_ref):
    n = 1024
    lane = lax.broadcasted_iota(jnp.int32, (8, n), 1)
    expert = lane // 16 * 4 + pair_ref[0]
    slot_of = lane // 8 % 2
    chunk = lane % 8
    sends = jnp.zeros((8, n), F32)
    weight = jnp.zeros((8, n), F32)
    for k in range(TOPK):
        hit = routes_ref[:, k : k + 1] == expert
        sends = jnp.where(hit, 1.0, sends)
        weight = jnp.where(hit, scale_ref[:, k : k + 1].astype(F32) / 32.0, weight)
    row = lax.broadcasted_iota(jnp.int32, (8, n), 0)
    slot = jnp.zeros((8, n), F32)
    for r in range(7):
        slot = slot + jnp.where(row > r, sends[r : r + 1, :], 0.0)
    keep = (sends > 0.0) & (slot == slot_of.astype(F32))
    sel = jnp.where(keep, 1.0, 0.0)
    wsel = jnp.where(keep, weight, 0.0)
    selects = []
    weights = []
    for c in range(8):
        selects.append(jnp.where(chunk == c, sel, 0.0))
        weights.append(jnp.where(chunk == c, wsel, 0.0))
    mt_ref[...] = jnp.concatenate(selects, axis=0).T.astype(BF16)
    w_ref[...] = jnp.concatenate(weights, axis=0).astype(BF16)


def dispatch_body(h_ref, gain_ref, mt_ref, out_ref):
    h = h_ref[...].astype(F32)
    h3 = h.reshape(8, 8, 256)
    sq = jnp.sum(jnp.sum(h3 * h3, axis=0), axis=1, keepdims=True)
    rs = lax.rsqrt(sq / D + 1e-05)
    normed = (h3 * rs[None] * gain_ref[...]).reshape(64, 256).astype(BF16)
    out_ref[...] = jnp.dot(mt_ref[...], normed, preferred_element_type=F32).astype(BF16)


def expert_body(x_ref, wgu_ref, wd_ref, out_ref, scr):
    for half in range(2):
        scr[half * 1024 : (half + 1) * 1024, :] = x_ref[:, half * 128 : (half + 1) * 128].astype(
            F32
        )
    acc = jnp.zeros((128, 512), F32)
    for c in range(8):
        xc = jnp.concatenate(
            [scr[pl.ds(half * 1024 + c, 128, stride=8), :] for half in range(2)], axis=1
        ).astype(BF16)
        acc = acc + jnp.dot(
            xc, wgu_ref[0, c * 256 : (c + 1) * 256, :], preferred_element_type=F32
        )
    act = (silu(acc[:, :256]) * acc[:, 256:]).astype(BF16)
    for c in range(8):
        o = jnp.dot(act, wd_ref[0, :, c * 256 : (c + 1) * 256], preferred_element_type=F32)
        for half in range(2):
            scr[pl.ds(half * 1024 + c, 128, stride=8), :] = o[:, half * 128 : (half + 1) * 128]
    for half in range(2):
        out_ref[:, half * 128 : (half + 1) * 128] = scr[
            half * 1024 : (half + 1) * 1024, :
        ].astype(BF16)


def combine_body(w_ref, x_ref, out_ref):
    out_ref[...] = jnp.dot(w_ref[...], x_ref[...], preferred_element_type=F32).astype(BF16)


def shape(dims, dtype=BF16):
    return jax.ShapeDtypeStruct(dims, dtype)


def a2a(x, axes):
    return lax.all_to_all(x, axes, split_axis=0, concat_axis=0, tiled=True)


def local(
    inputs,
    in_gain,
    w_qkvz,
    w_ab,
    a_log,
    dt_bias,
    state_values,
    state_scales,
    norm_gain,
    w_out,
    post_gain,
    routes,
    route_scale,
    w_gate_up,
    w_down,
):
    pair = (lax.axis_index("sub") // 2).astype(jnp.int32).reshape(1)
    sv = state_values.reshape(16, 128, 128)
    ss = state_scales.reshape(16, 128)
    part = call(
        project_body,
        shape((128, 768)),
        [VM] * 4,
        (inputs, in_gain.reshape(1, 256), w_qkvz, w_ab.T),
    )
    part = a2a(part, "sub")
    mt, wsel = call(
        route_body,
        (shape((1024, 64)), shape((64, 1024))),
        [SM, VM, VM],
        (pair, routes, route_scale),
    )
    gated, keys, delta, sd = call(
        recur_body,
        (shape((16, 128)), shape((16, 128), F32), shape((16, 128), F32), shape((16, 128), F32)),
        [VM, SM, SM, VM, VM, VM],
        (part, a_log, dt_bias, sv, ss, norm_gain.reshape(1, 128)),
    )
    gathered = a2a(jnp.broadcast_to(gated[None], (8, 16, 128)), "sub").reshape(128, 128)
    new_values, new_scales = call(
        state_body,
        (shape((16, 128, 128)), shape((16, 128), F32)),
        [VM] * 4,
        (sv, sd, keys, delta),
    )
    attn = jnp.dot(gathered, w_out, preferred_element_type=F32).astype(BF16)
    attn = a2a(attn, "head").reshape(16, 8, 256)
    attn = jnp.sum(attn.astype(F32), axis=0)
    resid = lax.dynamic_slice_in_dim(inputs, lax.axis_index("head") * 8, 8, 0).astype(F32)
    hidden = (resid + attn).astype(BF16)
    whole = a2a(jnp.broadcast_to(hidden[None], (8, 8, 256)), "sub").reshape(64, 256)
    buffer = call(
        dispatch_body,
        shape((1024, 256)),
        [VM] * 3,
        (whole, post_gain.reshape(8, 1, 256), mt),
    )
    received = a2a(buffer.reshape(64, 16, 256), ("grp", "head")).reshape(1024, 256)
    result = call(
        expert_body,
        shape((1024, 256)),
        [VM] * 3,
        (received, w_gate_up, w_down),
        [pltpu.VMEM((2048, 128), F32)],
    )
    back = a2a(result.reshape(64, 16, 256), ("grp", "head")).reshape(1024, 256)
    moe = call(combine_body, shape((64, 256)), [VM] * 2, (wsel, back))
    moe = a2a(moe.reshape(8, 8, 256), "sub")
    moe = jnp.sum(moe.astype(F32), axis=0)
    out = (hidden.astype(F32) + moe).astype(BF16)
    return (out, new_values.reshape(16, 1, 128, 128), new_scales.reshape(16, 1, 128))


def solution(mesh):
    placed = (
        P("grp", "sub"),
        P("sub"),
        P("sub", "head"),
        P("sub", "head"),
        P("head"),
        P("head"),
        P(("grp", "sub"), "head", None, None),
        P(("grp", "sub"), "head", None),
        P(),
        P("head", "sub"),
        P(),
        P(("grp", "head"), None),
        P(("grp", "head"), None),
        P(("grp", "head", "sub"), None, None),
        P(("grp", "head", "sub"), None, None),
    )
    return jax.shard_map(
        local,
        mesh=mesh,
        in_specs=placed,
        out_specs=(
            P(("grp", "head"), "sub"),
            P(("grp", "sub"), "head", None, None),
            P(("grp", "sub"), "head", None),
        ),
        check_vma=False,
    )
```

```python
import jax
import jax.numpy as jnp
from jax import lax
from jax.experimental import pallas as pl
from jax.experimental.pallas import tpu as pltpu
from jax.sharding import PartitionSpec as P

D = 2048
HD = 128
TOPK = 10
F32 = jnp.float32
BF16 = jnp.bfloat16

VM = pl.BlockSpec(memory_space=pltpu.VMEM)
SM = pl.BlockSpec(memory_space=pltpu.SMEM)
HB = pl.BlockSpec(memory_space=pltpu.HBM)
KEEP = pl.BlockSpec(memory_space=pltpu.HBM)


class Fetched:
    def __init__(self, src, dst, sem):
        self.copy = pltpu.make_async_copy(src, dst, sem)
        self.copy.start()
        self.dst = dst
        self.done = False

    def get(self):
        if not self.done:
            self.copy.wait()
            self.done = True
        return self.dst


def call(body, outs, ins, operands, scratch=(), vmem=32 << 20):
    fetched = [i for i, spec in enumerate(ins) if spec is HB]
    buffers = [pltpu.VMEM(operands[i].shape, operands[i].dtype) for i in fetched]

    def kernel(*refs):
        refs = list(refs)
        if fetched:
            sems = refs.pop()
            dsts = refs[len(refs) - len(fetched) :]
            refs = refs[: len(refs) - len(fetched)]
            for j, i in enumerate(fetched):
                refs[i] = Fetched(refs[i], dsts[j], sems.at[j])
        body(*refs)

    operands = [
        pltpu.with_memory_space_constraint(o, pltpu.HBM) if ins[i] is HB or ins[i] is KEEP else o
        for i, o in enumerate(operands)
    ]
    extra = buffers + ([pltpu.SemaphoreType.DMA((len(fetched),))] if fetched else [])
    return pl.pallas_call(
        kernel,
        out_shape=outs,
        in_specs=ins,
        out_specs=jax.tree.map(lambda _: VM, outs),
        scratch_shapes=list(scratch) + extra,
        compiler_params=pltpu.CompilerParams(vmem_limit_bytes=vmem),
    )(*operands)


def split_hi(x):
    hi = x.astype(BF16).astype(F32)
    return hi, x - hi


def project_body(sub_ref, head_ref, x_in, gain_in, w_in, wab_in, *rest):
    held, outs, resid_ref, kept, scr, sems = rest[:5], rest[5:13], rest[13], rest[14:19], rest[19], rest[20]
    copies = [pltpu.make_async_copy(held[i], kept[i], sems.at[i]) for i in range(5)]
    for copy in copies:
        copy.start()
    x_ref = x_in.get()
    xf = x_ref[...].astype(F32)
    xg = (xf * gain_in.get()[...]).astype(BF16)
    head = head_ref[0]
    start = pl.multiple_of(lax.div(head, 2) * 16, 16)
    near = x_ref[pl.ds(start, 16), :].astype(F32)
    resid_ref[...] = jnp.where(lax.rem(head, 2) == 1, near[8:], near[:8])
    wab_ref = wab_in.get()
    xgf = xg.astype(F32)
    a = jnp.sum(xgf * wab_ref[0:1, :].astype(F32), axis=1, keepdims=True)
    b = jnp.sum(xgf * wab_ref[1:2, :].astype(F32), axis=1, keepdims=True)
    s = jnp.sum(xf * xf, axis=1, keepdims=True)
    lane = lax.broadcasted_iota(jnp.int32, (xf.shape[0], 128), 1)
    tail = jnp.zeros((xf.shape[0], 128), F32)
    at = 0
    for v in (a, b, s):
        hi, lo = split_hi(v)
        tail = jnp.where(lane == at, hi, tail)
        tail = jnp.where(lane == at + 1, lo, tail)
        at += 2
    scr[:, 640:] = tail.astype(BF16)
    proj = jnp.dot(xg, w_in.get()[...], preferred_element_type=F32)
    key_hi, key_lo = split_hi(proj[:, 128:256])
    scr[:, :128] = proj[:, :128].astype(BF16)
    scr[:, 128:256] = key_hi.astype(BF16)
    scr[:, 256:512] = proj[:, 256:].astype(BF16)
    scr[:, 512:640] = key_lo.astype(BF16)
    for k in range(8):
        to = lax.rem(sub_ref[0] + k, 8)
        outs[k][...] = scr[pl.ds(pl.multiple_of(to * 16, 16), 16), :]
    for copy in copies:
        copy.wait()


def silu(x):
    return x * jax.nn.sigmoid(x)


def recur_body(*refs):
    parts = refs[:8]
    alog_ref, bias_ref, sv_ref, ss_ref, gain_ref, gated_ref, keys_ref, delta_ref, sd_ref = refs[8:]
    rows = 16
    t = parts[0][...].astype(F32)
    for i in range(1, 8):
        t = t + parts[i][...].astype(F32)
    tail = t[:, 640:]
    lane = lax.broadcasted_iota(jnp.int32, (rows, 128), 1)

    def column(i):
        return jnp.sum(
            jnp.where((lane == i) | (lane == i + 1), tail, 0.0), axis=1, keepdims=True
        )

    scale = lax.rsqrt(column(4) / D + 1e-05)
    proj = t[:, :512] * scale
    av = column(0) * scale
    bv = column(2) * scale
    query = silu(proj[:, :128])
    keys = silu(proj[:, 128:256] + t[:, 512:640] * scale)
    value = silu(proj[:, 256:384])
    zgate = proj[:, 384:512]
    query = (
        query
        * lax.rsqrt(jnp.sum(query * query, axis=-1, keepdims=True) + 1e-06)
        * (1.0 / 128.0**0.5)
    )
    keys = keys * lax.rsqrt(jnp.sum(keys * keys, axis=-1, keepdims=True) + 1e-06)
    beta = jax.nn.sigmoid(bv)
    rate = jnp.exp(jnp.zeros((1, 1), F32) + alog_ref[0])
    pre = av + bias_ref[0]
    soft = jnp.maximum(pre, 0.0) + jnp.log(1.0 + jnp.exp(-jnp.abs(pre)))
    decay = jnp.exp(-rate * soft)
    sd = ss_ref[...] * decay
    kd = (keys * sd).T
    qd = (query * sd).T
    mems = []
    cores = []
    for r in range(rows):
        v = sv_ref[r].astype(F32)
        mems.append(jnp.sum(v * kd[:, r : r + 1], axis=0, keepdims=True))
        cores.append(jnp.sum(v * qd[:, r : r + 1], axis=0, keepdims=True))
    memory = jnp.concatenate(mems, axis=0)
    core0 = jnp.concatenate(cores, axis=0)
    delta = (value - memory) * beta
    core = core0 + jnp.sum(query * keys, axis=-1, keepdims=True) * delta
    gated = (
        core
        * lax.rsqrt(jnp.mean(core * core, axis=-1, keepdims=True) + 1e-06)
        * gain_ref[...]
        * silu(zgate)
    )
    gated_ref[...] = gated.astype(BF16)
    keys_ref[...] = keys
    delta_ref[...] = delta
    sd_ref[...] = sd


def state_body(sv_ref, sd_ref, keys_ref, delta_ref, nv_ref, ns_ref):
    rows = 16
    sdt = sd_ref[...].T
    kt = keys_ref[...].T
    lane = lax.broadcasted_iota(jnp.int32, (128, rows), 1)
    peaks = jnp.zeros((128, rows), F32)
    for r in range(rows):
        s = sv_ref[r].astype(F32) * sdt[:, r : r + 1] + kt[:, r : r + 1] * delta_ref[r : r + 1, :]
        peak = jnp.max(jnp.abs(s), axis=1, keepdims=True) + 1e-06
        nv_ref[r] = (s / peak).astype(BF16)
        peaks = jnp.where(lane == r, peak, peaks)
    ns_ref[...] = peaks.T


def route_body(pair_ref, routes_in, scale_in, mt_ref, w_ref):
    routes_ref, scale_ref = routes_in.get(), scale_in.get()
    n = 1024
    lane = lax.broadcasted_iota(jnp.int32, (8, n), 1)
    expert = lane // 16 * 4 + pair_ref[0]
    slot_of = lane // 8 % 2
    chunk = lane % 8
    sends = jnp.zeros((8, n), F32)
    weight = jnp.zeros((8, n), F32)
    for k in range(TOPK):
        hit = routes_ref[:, k : k + 1] == expert
        sends = jnp.where(hit, 1.0, sends)
        weight = jnp.where(hit, scale_ref[:, k : k + 1].astype(F32) / 32.0, weight)
    row = lax.broadcasted_iota(jnp.int32, (8, n), 0)
    slot = jnp.zeros((8, n), F32)
    for r in range(7):
        slot = slot + jnp.where(row > r, sends[r : r + 1, :], 0.0)
    keep = (sends > 0.0) & (slot == slot_of.astype(F32))
    sel = jnp.where(keep, 1.0, 0.0)
    wsel = jnp.where(keep, weight, 0.0)
    selects = []
    weights = []
    for c in range(8):
        selects.append(jnp.where(chunk == c, sel, 0.0))
        weights.append(jnp.where(chunk == c, wsel, 0.0))
    mt_ref[...] = jnp.concatenate(selects, axis=0).T.astype(BF16)
    w_ref[...] = jnp.concatenate(weights, axis=0).astype(BF16)


def outproj_body(sub_ref, *refs):
    parts, w_ref, out_ref, scr = refs[:8], refs[8], refs[9], refs[10]
    for k in range(8):
        source = lax.rem(sub_ref[0] + 8 - k, 8)
        scr[pl.ds(pl.multiple_of(source * 16, 16), 16), :] = parts[k][...]
    out_ref[...] = jnp.dot(scr[...], w_ref[...], preferred_element_type=F32).astype(BF16)


def hidden_body(attn_ref, resid_ref, out_ref):
    attn = jnp.sum(attn_ref[...].astype(F32), axis=0)
    out_ref[...] = (resid_ref[...] + attn).astype(BF16)


def dispatch_body(sub_ref, *refs):
    parts, gain_ref, mt_ref, out_ref, scr = refs[:8], refs[8], refs[9], refs[10], refs[11]
    for k in range(8):
        source = lax.rem(sub_ref[0] + 8 - k, 8)
        scr[pl.ds(pl.multiple_of(source * 8, 8), 8), :] = parts[k][...].astype(F32)
    h3 = scr[...].reshape(8, 8, 256)
    sq = jnp.sum(jnp.sum(h3 * h3, axis=0), axis=1, keepdims=True)
    rs = lax.rsqrt(sq / D + 1e-05)
    normed = (h3 * rs[None] * gain_ref[...]).reshape(64, 256).astype(BF16)
    out_ref[...] = jnp.dot(mt_ref[...], normed, preferred_element_type=F32).astype(BF16)


def expert_body(x_ref, wgu_ref, wd_ref, out_ref, scr):
    for half in range(2):
        scr[half * 1024 : (half + 1) * 1024, :] = x_ref[:, half * 128 : (half + 1) * 128].astype(
            F32
        )
    acc = jnp.zeros((128, 512), F32)
    for c in range(8):
        xc = jnp.concatenate(
            [scr[pl.ds(half * 1024 + c, 128, stride=8), :] for half in range(2)], axis=1
        ).astype(BF16)
        acc = acc + jnp.dot(
            xc, wgu_ref[0, c * 256 : (c + 1) * 256, :], preferred_element_type=F32
        )
    act = (silu(acc[:, :256]) * acc[:, 256:]).astype(BF16)
    for c in range(8):
        o = jnp.dot(act, wd_ref[0, :, c * 256 : (c + 1) * 256], preferred_element_type=F32)
        for half in range(2):
            scr[pl.ds(half * 1024 + c, 128, stride=8), :] = o[:, half * 128 : (half + 1) * 128]
    for half in range(2):
        out_ref[:, half * 128 : (half + 1) * 128] = scr[
            half * 1024 : (half + 1) * 1024, :
        ].astype(BF16)


def combine_body(sub_ref, w_ref, x_ref, *rest):
    outs, scr = rest[:8], rest[8]
    scr[...] = jnp.dot(w_ref[...], x_ref[...], preferred_element_type=F32)
    for k in range(8):
        to = lax.rem(sub_ref[0] + k, 8)
        outs[k][...] = scr[pl.ds(pl.multiple_of(to * 8, 8), 8), :].astype(BF16)


def final_body(h_ref, *refs):
    parts, out_ref = refs[:8], refs[8]
    moe = parts[0][...].astype(F32)
    for k in range(1, 8):
        moe = moe + parts[k][...].astype(F32)
    out_ref[...] = (h_ref[...].astype(F32) + moe).astype(BF16)


def shape(dims, dtype=BF16):
    return jax.ShapeDtypeStruct(dims, dtype)


def a2a(x, axes):
    return lax.all_to_all(x, axes, split_axis=0, concat_axis=0, tiled=True)


def exchange(pieces):
    n = len(pieces)
    return [pieces[0]] + [
        lax.ppermute(pieces[k], "sub", [(i, (i + k) % n) for i in range(n)]) for k in range(1, n)
    ]


def local(
    inputs,
    in_gain,
    w_qkvz,
    w_ab,
    a_log,
    dt_bias,
    state_values,
    state_scales,
    norm_gain,
    w_out,
    post_gain,
    routes,
    route_scale,
    w_gate_up,
    w_down,
):
    sub = lax.axis_index("sub").astype(jnp.int32).reshape(1)
    head = lax.axis_index("head").astype(jnp.int32).reshape(1)
    sv = state_values.reshape(16, 128, 128)
    ss = state_scales.reshape(16, 128)
    part = call(
        project_body,
        (shape((16, 768)),) * 8
        + (
            shape((8, 256), F32),
            shape((16, 128, 128)),
            shape((16, 128), F32),
            shape((1, 128), F32),
            shape((128, 256)),
            shape((8, 1, 256), F32),
        ),
        [SM, SM, HB, HB, HB, HB] + [KEEP] * 5,
        (
            sub,
            head,
            inputs,
            in_gain.reshape(1, 256),
            w_qkvz,
            w_ab.T,
            sv,
            ss,
            norm_gain.reshape(1, 128),
            w_out,
            post_gain.reshape(8, 1, 256),
        ),
        [pltpu.VMEM((128, 768), BF16), pltpu.SemaphoreType.DMA((5,))],
    )
    part, (resid, sv, ss, ngain, w_out, pgain) = part[:8], part[8:]
    part = exchange(part)
    mt, wsel = call(
        route_body,
        (shape((1024, 64)), shape((64, 1024))),
        [SM, HB, HB],
        (sub // 2, routes, route_scale),
    )
    gated, keys, delta, sd = call(
        recur_body,
        (shape((16, 128)), shape((16, 128), F32), shape((16, 128), F32), shape((16, 128), F32)),
        [VM] * 8 + [SM, SM, VM, VM, VM],
        (*part, a_log, dt_bias, sv, ss, ngain),
    )
    gathered = exchange([gated] * 8)
    new_values, new_scales = call(
        state_body,
        (shape((16, 128, 128)), shape((16, 128), F32)),
        [VM] * 4,
        (sv, sd, keys, delta),
    )
    attn = call(
        outproj_body,
        shape((128, 256)),
        [SM] + [VM] * 9,
        (sub, *gathered, w_out),
        [pltpu.VMEM((128, 128), BF16)],
    )
    attn = a2a(attn.reshape(16, 8, 256), "head")
    hidden = call(hidden_body, shape((8, 256)), [VM, VM], (attn, resid))
    whole = exchange([hidden] * 8)
    buffer = call(
        dispatch_body,
        shape((1024, 256)),
        [SM] + [VM] * 10,
        (sub, *whole, pgain, mt),
        [pltpu.VMEM((64, 256), F32)],
    )
    received = a2a(buffer.reshape(64, 16, 256), ("grp", "head")).reshape(1024, 256)
    result = call(
        expert_body,
        shape((1024, 256)),
        [VM] * 3,
        (received, w_gate_up, w_down),
        [pltpu.VMEM((2048, 128), F32)],
    )
    back = a2a(result.reshape(64, 16, 256), ("grp", "head")).reshape(1024, 256)
    moe = call(
        combine_body,
        (shape((8, 256)),) * 8,
        [SM, VM, VM],
        (sub, wsel, back),
        [pltpu.VMEM((64, 256), F32)],
    )
    moe = exchange(moe)
    out = call(final_body, shape((8, 256)), [VM] * 9, (hidden, *moe))
    return (out, new_values.reshape(16, 1, 128, 128), new_scales.reshape(16, 1, 128))


def solution(mesh):
    placed = (
        P("grp", "sub"),
        P("sub"),
        P("sub", "head"),
        P("sub", "head"),
        P("head"),
        P("head"),
        P(("grp", "sub"), "head", None, None),
        P(("grp", "sub"), "head", None),
        P(),
        P("head", "sub"),
        P(),
        P(("grp", "head"), None),
        P(("grp", "head"), None),
        P(("grp", "head", "sub"), None, None),
        P(("grp", "head", "sub"), None, None),
    )
    return jax.shard_map(
        local,
        mesh=mesh,
        in_specs=placed,
        out_specs=(
            P(("grp", "head"), "sub"),
            P(("grp", "sub"), "head", None, None),
            P(("grp", "sub"), "head", None),
        ),
        check_vma=False,
    )
```

```python
import jax
import jax.numpy as jnp
from jax import lax
from jax.experimental import pallas as pl
from jax.experimental.pallas import tpu as pltpu
from jax.sharding import PartitionSpec as P

D = 2048
HD = 128
TOPK = 10
F32 = jnp.float32
BF16 = jnp.bfloat16

VM = pl.BlockSpec(memory_space=pltpu.VMEM)
SM = pl.BlockSpec(memory_space=pltpu.SMEM)
HB = pl.BlockSpec(memory_space=pltpu.HBM)
KEEP = pl.BlockSpec(memory_space=pltpu.HBM)


class Fetched:
    def __init__(self, src, dst, sem):
        self.copy = pltpu.make_async_copy(src, dst, sem)
        self.copy.start()
        self.dst = dst
        self.done = False

    def get(self):
        if not self.done:
            self.copy.wait()
            self.done = True
        return self.dst


def call(body, outs, ins, operands, scratch=(), vmem=32 << 20):
    fetched = [i for i, spec in enumerate(ins) if spec is HB]
    buffers = [pltpu.VMEM(operands[i].shape, operands[i].dtype) for i in fetched]

    def kernel(*refs):
        refs = list(refs)
        if fetched:
            sems = refs.pop()
            dsts = refs[len(refs) - len(fetched) :]
            refs = refs[: len(refs) - len(fetched)]
            for j, i in enumerate(fetched):
                refs[i] = Fetched(refs[i], dsts[j], sems.at[j])
        body(*refs)

    operands = [
        pltpu.with_memory_space_constraint(o, pltpu.HBM) if ins[i] is HB or ins[i] is KEEP else o
        for i, o in enumerate(operands)
    ]
    extra = buffers + ([pltpu.SemaphoreType.DMA((len(fetched),))] if fetched else [])
    return pl.pallas_call(
        kernel,
        out_shape=outs,
        in_specs=ins,
        out_specs=jax.tree.map(lambda _: VM, outs),
        scratch_shapes=list(scratch) + extra,
        compiler_params=pltpu.CompilerParams(vmem_limit_bytes=vmem),
    )(*operands)


def split_hi(x):
    hi = x.astype(BF16).astype(F32)
    return hi, x - hi


def project_body(head_ref, x_in, gain_in, w_in, wab_in, *rest):
    held, out_ref, resid_ref, kept, sems = rest[:5], rest[5], rest[6], rest[7:12], rest[12]
    copies = [pltpu.make_async_copy(held[i], kept[i], sems.at[i]) for i in range(5)]
    for copy in copies:
        copy.start()
    x_ref = x_in.get()
    xf = x_ref[...].astype(F32)
    xg = (xf * gain_in.get()[...]).astype(BF16)
    head = head_ref[0]
    start = pl.multiple_of(lax.div(head, 2) * 16, 16)
    near = x_ref[pl.ds(start, 16), :].astype(F32)
    resid_ref[...] = jnp.where(lax.rem(head, 2) == 1, near[8:], near[:8])
    wab_ref = wab_in.get()
    xgf = xg.astype(F32)
    a = jnp.sum(xgf * wab_ref[0:1, :].astype(F32), axis=1, keepdims=True)
    b = jnp.sum(xgf * wab_ref[1:2, :].astype(F32), axis=1, keepdims=True)
    s = jnp.sum(xf * xf, axis=1, keepdims=True)
    lane = lax.broadcasted_iota(jnp.int32, (xf.shape[0], 128), 1)
    tail = jnp.zeros((xf.shape[0], 128), F32)
    at = 0
    for v in (a, b, s):
        hi, lo = split_hi(v)
        tail = jnp.where(lane == at, hi, tail)
        tail = jnp.where(lane == at + 1, lo, tail)
        at += 2
    out_ref[:, 640:] = tail.astype(BF16)
    proj = jnp.dot(xg, w_in.get()[...], preferred_element_type=F32)
    key_hi, key_lo = split_hi(proj[:, 128:256])
    out_ref[:, :128] = proj[:, :128].astype(BF16)
    out_ref[:, 128:256] = key_hi.astype(BF16)
    out_ref[:, 256:512] = proj[:, 256:].astype(BF16)
    out_ref[:, 512:640] = key_lo.astype(BF16)
    for copy in copies:
        copy.wait()


def silu(x):
    return x * jax.nn.sigmoid(x)


def recur_body(
    p_ref, alog_ref, bias_ref, sv_ref, ss_ref, gain_ref, gated_ref, keys_ref, delta_ref, sd_ref
):
    rows = 16
    t = p_ref[0].astype(F32)
    for i in range(1, 8):
        t = t + p_ref[i].astype(F32)
    tail = t[:, 640:]
    lane = lax.broadcasted_iota(jnp.int32, (rows, 128), 1)

    def column(i):
        return jnp.sum(
            jnp.where((lane == i) | (lane == i + 1), tail, 0.0), axis=1, keepdims=True
        )

    scale = lax.rsqrt(column(4) / D + 1e-05)
    proj = t[:, :512] * scale
    av = column(0) * scale
    bv = column(2) * scale
    query = silu(proj[:, :128])
    keys = silu(proj[:, 128:256] + t[:, 512:640] * scale)
    value = silu(proj[:, 256:384])
    zgate = proj[:, 384:512]
    query = (
        query
        * lax.rsqrt(jnp.sum(query * query, axis=-1, keepdims=True) + 1e-06)
        * (1.0 / 128.0**0.5)
    )
    keys = keys * lax.rsqrt(jnp.sum(keys * keys, axis=-1, keepdims=True) + 1e-06)
    beta = jax.nn.sigmoid(bv)
    rate = jnp.exp(jnp.zeros((1, 1), F32) + alog_ref[0])
    pre = av + bias_ref[0]
    soft = jnp.maximum(pre, 0.0) + jnp.log(1.0 + jnp.exp(-jnp.abs(pre)))
    decay = jnp.exp(-rate * soft)
    sd = ss_ref[...] * decay
    kd = (keys * sd).T
    qd = (query * sd).T
    mems = []
    cores = []
    for r in range(rows):
        v = sv_ref[r].astype(F32)
        mems.append(jnp.sum(v * kd[:, r : r + 1], axis=0, keepdims=True))
        cores.append(jnp.sum(v * qd[:, r : r + 1], axis=0, keepdims=True))
    memory = jnp.concatenate(mems, axis=0)
    core0 = jnp.concatenate(cores, axis=0)
    delta = (value - memory) * beta
    core = core0 + jnp.sum(query * keys, axis=-1, keepdims=True) * delta
    gated = (
        core
        * lax.rsqrt(jnp.mean(core * core, axis=-1, keepdims=True) + 1e-06)
        * gain_ref[...]
        * silu(zgate)
    )
    gated = gated.astype(BF16)
    for i in range(8):
        gated_ref[i] = gated
    keys_ref[...] = keys
    delta_ref[...] = delta
    sd_ref[...] = sd


def state_body(sv_ref, sd_ref, keys_ref, delta_ref, nv_ref, ns_ref):
    rows = 16
    sdt = sd_ref[...].T
    kt = keys_ref[...].T
    lane = lax.broadcasted_iota(jnp.int32, (128, rows), 1)
    peaks = jnp.zeros((128, rows), F32)
    for r in range(rows):
        s = sv_ref[r].astype(F32) * sdt[:, r : r + 1] + kt[:, r : r + 1] * delta_ref[r : r + 1, :]
        peak = jnp.max(jnp.abs(s), axis=1, keepdims=True) + 1e-06
        nv_ref[r] = (s / peak).astype(BF16)
        peaks = jnp.where(lane == r, peak, peaks)
    ns_ref[...] = peaks.T


def route_body(routes_in, scale_in, mt_ref, w_ref):
    routes_ref, scale_ref = routes_in.get(), scale_in.get()
    n = 2048
    lane = lax.broadcasted_iota(jnp.int32, (8, n), 1)
    expert = lane // 8
    slot_of = lane // 2 % 2
    half = lane % 2
    sends = jnp.zeros((8, n), F32)
    weight = jnp.zeros((8, n), F32)
    for k in range(TOPK):
        hit = routes_ref[:, k : k + 1] == expert
        sends = jnp.where(hit, 1.0, sends)
        weight = jnp.where(hit, scale_ref[:, k : k + 1].astype(F32) / 32.0, weight)
    row = lax.broadcasted_iota(jnp.int32, (8, n), 0)
    slot = jnp.zeros((8, n), F32)
    for r in range(7):
        slot = slot + jnp.where(row > r, sends[r : r + 1, :], 0.0)
    keep = (sends > 0.0) & (slot == slot_of.astype(F32))
    sel = jnp.where(keep, 1.0, 0.0)
    wsel = jnp.where(keep, weight, 0.0)
    first = half == 0
    selects = [jnp.where(first, sel, 0.0), jnp.where(first, 0.0, sel)]
    weights = [jnp.where(first, wsel, 0.0), jnp.where(first, 0.0, wsel)]
    mt_ref[...] = jnp.concatenate(selects, axis=0).T.astype(BF16)
    w_ref[...] = jnp.concatenate(weights, axis=0).astype(BF16)


def outproj_body(x_ref, w_ref, out_ref):
    out_ref[...] = jnp.dot(x_ref[...], w_ref[...], preferred_element_type=F32).astype(BF16)


def dispatch_body(attn_ref, resid_ref, mt_ref, hidden_ref, out_ref):
    attn = jnp.sum(attn_ref[...].astype(F32), axis=0)
    hidden = (resid_ref[...] + attn).astype(BF16)
    hidden_ref[...] = hidden
    hf = hidden.astype(F32)
    halves = jnp.concatenate([hf[:, :128], hf[:, 128:]], axis=0).astype(BF16)
    sent = jnp.dot(mt_ref[...], halves, preferred_element_type=F32)
    out_ref[...] = sent.reshape(512, 4, 128).astype(BF16)


def expert_body(x_ref, gain_ref, wgu_ref, wd_ref, out_ref, scr):
    scr[...] = x_ref[...].astype(F32).reshape(2048, 128)

    def rows_of(c, slot, half):
        return pl.ds(c * 4 + slot * 2 + half, 64, stride=32)

    chunks = []
    sq = jnp.zeros((128, 128), F32)
    for c in range(8):
        halves = [
            jnp.concatenate([scr[rows_of(c, slot, half), :] for slot in range(2)], axis=0)
            for half in range(2)
        ]
        sq = sq + halves[0] * halves[0] + halves[1] * halves[1]
        chunks.append(jnp.concatenate(halves, axis=1))
    rs = lax.rsqrt(jnp.sum(sq, axis=1, keepdims=True) / D + 1e-05)
    acc = jnp.zeros((128, 512), F32)
    for c in range(8):
        xc = (chunks[c] * rs * gain_ref[c]).astype(BF16)
        acc = acc + jnp.dot(
            xc, wgu_ref[0, c * 256 : (c + 1) * 256, :], preferred_element_type=F32
        )
    act = (silu(acc[:, :256]) * acc[:, 256:]).astype(BF16)
    for c in range(8):
        o = jnp.dot(act, wd_ref[0, :, c * 256 : (c + 1) * 256], preferred_element_type=F32)
        for slot in range(2):
            for half in range(2):
                scr[rows_of(c, slot, half), :] = o[
                    slot * 64 : (slot + 1) * 64, half * 128 : (half + 1) * 128
                ]
    out_ref[...] = scr[...].reshape(512, 4, 128).astype(BF16)


def combine_body(w_ref, x_ref, hidden_ref, out_ref):
    x = x_ref[...].astype(F32).reshape(2048, 128).astype(BF16)
    moe = jnp.dot(w_ref[...], x, preferred_element_type=F32)
    moe = jnp.concatenate([moe[:8], moe[8:]], axis=1)
    out_ref[...] = (hidden_ref[...].astype(F32) + moe).astype(BF16)


def shape(dims, dtype=BF16):
    return jax.ShapeDtypeStruct(dims, dtype)


def a2a(x, axes):
    return lax.all_to_all(x, axes, split_axis=0, concat_axis=0, tiled=True)


def local(
    inputs,
    in_gain,
    w_qkvz,
    w_ab,
    a_log,
    dt_bias,
    state_values,
    state_scales,
    norm_gain,
    w_out,
    post_gain,
    routes,
    route_scale,
    w_gate_up,
    w_down,
):
    head = lax.axis_index("head").astype(jnp.int32).reshape(1)
    sv = state_values.reshape(16, 128, 128)
    ss = state_scales.reshape(16, 128)
    part, resid, sv, ss, ngain, w_out, pgain = call(
        project_body,
        (
            shape((128, 768)),
            shape((8, 256), F32),
            shape((16, 128, 128)),
            shape((16, 128), F32),
            shape((1, 128), F32),
            shape((128, 256)),
            shape((8, 1, 256), F32),
        ),
        [SM, HB, HB, HB, HB] + [KEEP] * 5,
        (
            head,
            inputs,
            in_gain.reshape(1, 256),
            w_qkvz,
            w_ab.T,
            sv,
            ss,
            norm_gain.reshape(1, 128),
            w_out,
            post_gain.reshape(8, 1, 256),
        ),
        [pltpu.SemaphoreType.DMA((5,))],
    )
    part = a2a(part.reshape(8, 16, 768), "sub")
    mt, wsel = call(
        route_body,
        (shape((2048, 16)), shape((16, 2048))),
        [HB, HB],
        (routes, route_scale),
    )
    gated, keys, delta, sd = call(
        recur_body,
        (shape((8, 16, 128)), shape((16, 128), F32), shape((16, 128), F32), shape((16, 128), F32)),
        [VM, SM, SM, VM, VM, VM],
        (part, a_log, dt_bias, sv, ss, ngain),
    )
    gathered = a2a(gated, "sub").reshape(128, 128)
    new_values, new_scales = call(
        state_body,
        (shape((16, 128, 128)), shape((16, 128), F32)),
        [VM] * 4,
        (sv, sd, keys, delta),
    )
    attn = call(outproj_body, shape((128, 256)), [VM] * 2, (gathered, w_out))
    attn = a2a(attn.reshape(16, 8, 256), "head")
    hidden, sent = call(
        dispatch_body,
        (shape((8, 256)), shape((512, 4, 128))),
        [VM] * 3,
        (attn, resid, mt),
    )
    every = ("grp", "head", "sub")
    received = a2a(sent, every)
    result = call(
        expert_body,
        shape((512, 4, 128)),
        [VM] * 4,
        (received, pgain, w_gate_up, w_down),
        [pltpu.VMEM((2048, 128), F32)],
    )
    back = a2a(result, every)
    out = call(combine_body, shape((8, 256)), [VM] * 3, (wsel, back, hidden))
    return (out, new_values.reshape(16, 1, 128, 128), new_scales.reshape(16, 1, 128))


def solution(mesh):
    placed = (
        P("grp", "sub"),
        P("sub"),
        P("sub", "head"),
        P("sub", "head"),
        P("head"),
        P("head"),
        P(("grp", "sub"), "head", None, None),
        P(("grp", "sub"), "head", None),
        P(),
        P("head", "sub"),
        P(),
        P(("grp", "head"), None),
        P(("grp", "head"), None),
        P(("grp", "head", "sub"), None, None),
        P(("grp", "head", "sub"), None, None),
    )
    return jax.shard_map(
        local,
        mesh=mesh,
        in_specs=placed,
        out_specs=(
            P(("grp", "head"), "sub"),
            P(("grp", "sub"), "head", None, None),
            P(("grp", "sub"), "head", None),
        ),
        check_vma=False,
    )
```

```python
import jax
import jax.numpy as jnp
from jax import lax
from jax.experimental import pallas as pl
from jax.experimental.pallas import tpu as pltpu
from jax.sharding import PartitionSpec as P

D = 2048
HD = 128
TOPK = 10
F32 = jnp.float32
BF16 = jnp.bfloat16
SUB = ("quad", "side")

VM = pl.BlockSpec(memory_space=pltpu.VMEM)
SM = pl.BlockSpec(memory_space=pltpu.SMEM)
HB = pl.BlockSpec(memory_space=pltpu.HBM)
KEEP = pl.BlockSpec(memory_space=pltpu.HBM)


class Fetched:
    def __init__(self, src, dst, sem):
        self.copy = pltpu.make_async_copy(src, dst, sem)
        self.copy.start()
        self.dst = dst
        self.done = False

    def get(self):
        if not self.done:
            self.copy.wait()
            self.done = True
        return self.dst


def call(body, outs, ins, operands, scratch=(), vmem=32 << 20):
    fetched = [i for i, spec in enumerate(ins) if spec is HB]
    buffers = [pltpu.VMEM(operands[i].shape, operands[i].dtype) for i in fetched]

    def kernel(*refs):
        refs = list(refs)
        if fetched:
            sems = refs.pop()
            dsts = refs[len(refs) - len(fetched) :]
            refs = refs[: len(refs) - len(fetched)]
            for j, i in enumerate(fetched):
                refs[i] = Fetched(refs[i], dsts[j], sems.at[j])
        body(*refs)

    operands = [
        pltpu.with_memory_space_constraint(o, pltpu.HBM) if ins[i] is HB or ins[i] is KEEP else o
        for i, o in enumerate(operands)
    ]
    extra = buffers + ([pltpu.SemaphoreType.DMA((len(fetched),))] if fetched else [])
    return pl.pallas_call(
        kernel,
        out_shape=outs,
        in_specs=ins,
        out_specs=jax.tree.map(lambda _: VM, outs),
        scratch_shapes=list(scratch) + extra,
        compiler_params=pltpu.CompilerParams(vmem_limit_bytes=vmem),
    )(*operands)


def split_hi(x):
    hi = x.astype(BF16).astype(F32)
    return hi, x - hi


def project_body(head_ref, x_in, gain_in, w_in, wab_in, out_ref, resid_ref):
    x_ref = x_in.get()
    xf = x_ref[...].astype(F32)
    xg = (xf * gain_in.get()[...]).astype(BF16)
    head = head_ref[0]
    start = pl.multiple_of(lax.div(head, 2) * 16, 16)
    near = x_ref[pl.ds(start, 16), :].astype(F32)
    resid_ref[...] = jnp.where(lax.rem(head, 2) == 1, near[8:], near[:8])
    wab_ref = wab_in.get()
    xgf = xg.astype(F32)
    a = jnp.sum(xgf * wab_ref[0:1, :].astype(F32), axis=1, keepdims=True)
    b = jnp.sum(xgf * wab_ref[1:2, :].astype(F32), axis=1, keepdims=True)
    s = jnp.sum(xf * xf, axis=1, keepdims=True)
    lane = lax.broadcasted_iota(jnp.int32, (xf.shape[0], 128), 1)
    tail = jnp.zeros((xf.shape[0], 128), F32)
    at = 0
    for v in (a, b, s):
        hi, lo = split_hi(v)
        tail = jnp.where(lane == at, hi, tail)
        tail = jnp.where(lane == at + 1, lo, tail)
        at += 2
    out_ref[:, 640:] = tail.astype(BF16)
    proj = jnp.dot(xg, w_in.get()[...], preferred_element_type=F32)
    key_hi, key_lo = split_hi(proj[:, 128:256])
    out_ref[:, :128] = proj[:, :128].astype(BF16)
    out_ref[:, 128:256] = key_hi.astype(BF16)
    out_ref[:, 256:512] = proj[:, 256:].astype(BF16)
    out_ref[:, 512:640] = key_lo.astype(BF16)

def silu(x):
    return x * jax.nn.sigmoid(x)


def recur_body(
    sub_ref, p_ref, alog_ref, bias_ref, sv_ref, ss_ref, gain_ref, gated_ref, keys_ref, delta_ref, sd_ref
):
    rows = 16
    t = p_ref[0].astype(F32)
    for i in range(1, 8):
        t = t + p_ref[i].astype(F32)
    tail = t[:, 640:]
    lane = lax.broadcasted_iota(jnp.int32, (rows, 128), 1)

    def column(i):
        return jnp.sum(
            jnp.where((lane == i) | (lane == i + 1), tail, 0.0), axis=1, keepdims=True
        )

    scale = lax.rsqrt(column(4) / D + 1e-05)
    proj = t[:, :512] * scale
    av = column(0) * scale
    bv = column(2) * scale
    query = silu(proj[:, :128])
    keys = silu(proj[:, 128:256] + t[:, 512:640] * scale)
    value = silu(proj[:, 256:384])
    zgate = proj[:, 384:512]
    query = (
        query
        * lax.rsqrt(jnp.sum(query * query, axis=-1, keepdims=True) + 1e-06)
        * (1.0 / 128.0**0.5)
    )
    keys = keys * lax.rsqrt(jnp.sum(keys * keys, axis=-1, keepdims=True) + 1e-06)
    beta = jax.nn.sigmoid(bv)
    rate = jnp.exp(jnp.zeros((1, 1), F32) + alog_ref[0])
    pre = av + bias_ref[0]
    soft = jnp.maximum(pre, 0.0) + jnp.log(1.0 + jnp.exp(-jnp.abs(pre)))
    decay = jnp.exp(-rate * soft)
    sd = ss_ref[...] * decay
    kd = (keys * sd).T
    qd = (query * sd).T
    mems = []
    cores = []
    for r in range(rows):
        v = sv_ref[r].astype(F32)
        mems.append(jnp.sum(v * kd[:, r : r + 1], axis=0, keepdims=True))
        cores.append(jnp.sum(v * qd[:, r : r + 1], axis=0, keepdims=True))
    memory = jnp.concatenate(mems, axis=0)
    core0 = jnp.concatenate(cores, axis=0)
    delta = (value - memory) * beta
    core = core0 + jnp.sum(query * keys, axis=-1, keepdims=True) * delta
    gated = (
        core
        * lax.rsqrt(jnp.mean(core * core, axis=-1, keepdims=True) + 1e-06)
        * gain_ref[...]
        * silu(zgate)
    )
    block = sub_ref[0] * 16
    for b in range(2):
        piece = gated[b * 8 : (b + 1) * 8].astype(BF16)
        for i in range(8):
            gated_ref[block + b * 8 + i] = piece
    keys_ref[...] = keys
    delta_ref[...] = delta
    sd_ref[...] = sd


def state_body(sv_ref, sd_ref, keys_ref, delta_ref, nv_ref, ns_ref):
    rows = 16
    sdt = sd_ref[...].T
    kt = keys_ref[...].T
    lane = lax.broadcasted_iota(jnp.int32, (128, rows), 1)
    peaks = jnp.zeros((128, rows), F32)
    for r in range(rows):
        s = sv_ref[r].astype(F32) * sdt[:, r : r + 1] + kt[:, r : r + 1] * delta_ref[r : r + 1, :]
        peak = jnp.max(jnp.abs(s), axis=1, keepdims=True) + 1e-06
        nv_ref[r] = (s / peak).astype(BF16)
        peaks = jnp.where(lane == r, peak, peaks)
    ns_ref[...] = peaks.T


def prepare_body(routes_in, scale_in, *rest):
    held, mt_ref, w_ref, kept, sems = rest[:4], rest[4], rest[5], rest[6:10], rest[10]
    copies = [pltpu.make_async_copy(held[i], kept[i], sems.at[i]) for i in range(4)]
    for copy in copies:
        copy.start()
    routes_ref, scale_ref = routes_in.get(), scale_in.get()
    n = 2048
    lane = lax.broadcasted_iota(jnp.int32, (8, n), 1)
    expert = lane // 8
    slot_of = lane // 4 % 2
    quarter = lane % 4
    sends = jnp.zeros((8, n), F32)
    weight = jnp.zeros((8, n), F32)
    for k in range(TOPK):
        hit = routes_ref[:, k : k + 1] == expert
        sends = jnp.where(hit, 1.0, sends)
        weight = jnp.where(hit, scale_ref[:, k : k + 1].astype(F32) / 32.0, weight)
    row = lax.broadcasted_iota(jnp.int32, (8, n), 0)
    slot = jnp.zeros((8, n), F32)
    for r in range(7):
        slot = slot + jnp.where(row > r, sends[r : r + 1, :], 0.0)
    keep = (sends > 0.0) & (slot == slot_of.astype(F32))
    sel = jnp.where(keep, 1.0, 0.0)
    wsel = jnp.where(keep, weight, 0.0)
    selects = [jnp.where(quarter == i, sel, 0.0) for i in range(4)]
    weights = [jnp.where(quarter == i, wsel, 0.0) for i in range(4)]
    mt_ref[...] = jnp.concatenate(selects, axis=0).T.astype(BF16)
    w_ref[...] = jnp.concatenate(weights, axis=0).astype(BF16)
    for copy in copies:
        copy.wait()


def hidden_body(head_ref, x_ref, resid_ref, w_in, hidden_ref):
    block = lax.div(head_ref[0], 2)
    gated = jnp.concatenate([x_ref[h * 8 + block].astype(F32) for h in range(16)], axis=1)
    attn = jnp.dot(gated.astype(BF16), w_in.get()[...], preferred_element_type=F32)
    hidden_ref[...] = (resid_ref[...] + attn).astype(BF16)


def dispatch_body(side_ref, mine_ref, other_ref, mt_ref, out_ref):
    first = side_ref[0] == 0
    mine = mine_ref[...].astype(F32)
    other = other_ref[...].astype(F32)
    lo = jnp.where(first, mine, other)
    hi = jnp.where(first, other, mine)
    quarters = jnp.concatenate(
        [lo[:, :128], lo[:, 128:], hi[:, :128], hi[:, 128:]], axis=0
    ).astype(BF16)
    out_ref[...] = jnp.dot(mt_ref[...], quarters, preferred_element_type=F32).astype(BF16)


def expert_body(x_ref, gain_ref, wgu_ref, wd_ref, out_ref, scr):
    scr[...] = x_ref[...].astype(F32)

    def rows_of(c, slot, half):
        return pl.ds(c // 2 * 8 + slot * 4 + c % 2 * 2 + half, 64, stride=32)

    chunks = []
    sq = jnp.zeros((128, 128), F32)
    for c in range(8):
        halves = [
            jnp.concatenate([scr[rows_of(c, slot, half), :] for slot in range(2)], axis=0)
            for half in range(2)
        ]
        sq = sq + halves[0] * halves[0] + halves[1] * halves[1]
        chunks.append(jnp.concatenate(halves, axis=1))
    rs = lax.rsqrt(jnp.sum(sq, axis=1, keepdims=True) / D + 1e-05)
    acc = jnp.zeros((128, 512), F32)
    for c in range(8):
        xc = (chunks[c] * rs * gain_ref[c]).astype(BF16)
        acc = acc + jnp.dot(
            xc, wgu_ref[0, c * 256 : (c + 1) * 256, :], preferred_element_type=F32
        )
    act = (silu(acc[:, :256]) * acc[:, 256:]).astype(BF16)
    for c in range(8):
        o = jnp.dot(act, wd_ref[0, :, c * 256 : (c + 1) * 256], preferred_element_type=F32)
        for slot in range(2):
            for half in range(2):
                scr[rows_of(c, slot, half), :] = o[
                    slot * 64 : (slot + 1) * 64, half * 128 : (half + 1) * 128
                ]
    out_ref[...] = scr[...].astype(BF16)


def combine_body(side_ref, w_ref, x_ref, hidden_ref, mine_ref, other_ref):
    first = side_ref[0] == 0
    moe = jnp.dot(w_ref[...], x_ref[...], preferred_element_type=F32)
    lo = jnp.concatenate([moe[:8], moe[8:16]], axis=1)
    hi = jnp.concatenate([moe[16:24], moe[24:]], axis=1)
    mine_ref[...] = hidden_ref[...].astype(F32) + jnp.where(first, lo, hi)
    other_ref[...] = jnp.where(first, hi, lo)


def final_body(mine_ref, other_ref, out_ref):
    out_ref[...] = (mine_ref[...] + other_ref[...]).astype(BF16)


def shape(dims, dtype=BF16):
    return jax.ShapeDtypeStruct(dims, dtype)


def a2a(x, axes):
    return lax.all_to_all(x, axes, split_axis=0, concat_axis=0, tiled=True)


def local(
    inputs,
    in_gain,
    w_qkvz,
    w_ab,
    a_log,
    dt_bias,
    state_values,
    state_scales,
    norm_gain,
    w_out,
    post_gain,
    routes,
    route_scale,
    w_gate_up,
    w_down,
):
    head = lax.axis_index("head").astype(jnp.int32).reshape(1)
    side = lax.axis_index("side").astype(jnp.int32).reshape(1)
    sub = lax.axis_index("quad").astype(jnp.int32).reshape(1) * 2 + side
    w_cols = lax.all_gather(w_out, "head", axis=0, tiled=True)
    part, resid = call(
        project_body,
        (shape((128, 768)), shape((8, 256), F32)),
        [SM, HB, HB, HB, HB],
        (head, inputs, in_gain.reshape(1, 256), w_qkvz, w_ab.T),
    )
    part = a2a(part.reshape(8, 16, 768), SUB)
    mt, wsel, sv, ss, ngain, pgain = call(
        prepare_body,
        (
            shape((2048, 32)),
            shape((32, 2048)),
            shape((16, 128, 128)),
            shape((16, 128), F32),
            shape((1, 128), F32),
            shape((8, 1, 256), F32),
        ),
        [HB, HB] + [KEEP] * 4,
        (
            routes,
            route_scale,
            state_values.reshape(16, 128, 128),
            state_scales.reshape(16, 128),
            norm_gain.reshape(1, 128),
            post_gain.reshape(8, 1, 256),
        ),
        [pltpu.SemaphoreType.DMA((4,))],
    )
    gated, keys, delta, sd = call(
        recur_body,
        (shape((128, 8, 128)), shape((16, 128), F32), shape((16, 128), F32), shape((16, 128), F32)),
        [SM, VM, SM, SM, VM, VM, VM],
        (sub, part, a_log, dt_bias, sv, ss, ngain),
    )
    gathered = a2a(gated, ("head",) + SUB)
    new_values, new_scales = call(
        state_body,
        (shape((16, 128, 128)), shape((16, 128), F32)),
        [VM] * 4,
        (sv, sd, keys, delta),
    )
    hidden = call(
        hidden_body, shape((8, 256)), [SM, VM, VM, HB], (head, gathered, resid, w_cols)
    )
    swap = [(0, 1), (1, 0)]
    neighbour = lax.ppermute(hidden, "side", swap)
    sent = call(
        dispatch_body, shape((2048, 128)), [SM, VM, VM, VM], (side, hidden, neighbour, mt)
    )
    halves = ("grp", "head", "quad")
    received = a2a(sent.reshape(256, 8, 128), halves).reshape(2048, 128)
    result = call(
        expert_body,
        shape((2048, 128)),
        [VM] * 4,
        (received, pgain, w_gate_up, w_down),
        [pltpu.VMEM((2048, 128), F32)],
    )
    back = a2a(result.reshape(256, 8, 128), halves).reshape(2048, 128)
    mine, other = call(
        combine_body,
        (shape((8, 256), F32), shape((8, 256), F32)),
        [SM] + [VM] * 3,
        (side, wsel, back, hidden),
    )
    other = lax.ppermute(other, "side", swap)
    out = call(final_body, shape((8, 256)), [VM, VM], (mine, other))
    return (out, new_values.reshape(16, 1, 128, 128), new_scales.reshape(16, 1, 128))


def solution(mesh):
    shape4 = (mesh.shape["grp"], mesh.shape["head"], mesh.shape["sub"] // 2, 2)
    mesh = jax.sharding.Mesh(mesh.devices.reshape(shape4), ("grp", "head") + SUB)
    placed = (
        P("grp", SUB),
        P(SUB),
        P(SUB, "head"),
        P(SUB, "head"),
        P("head"),
        P("head"),
        P(("grp",) + SUB, "head", None, None),
        P(("grp",) + SUB, "head", None),
        P(),
        P("head", SUB),
        P(),
        P(("grp", "head"), None),
        P(("grp", "head"), None),
        P(("grp", "head") + SUB, None, None),
        P(("grp", "head") + SUB, None, None),
    )
    return jax.shard_map(
        local,
        mesh=mesh,
        in_specs=placed,
        out_specs=(
            P(("grp", "head"), SUB),
            P(("grp",) + SUB, "head", None, None),
            P(("grp",) + SUB, "head", None),
        ),
        check_vma=False,
    )
```

```python
import jax
import jax.numpy as jnp
from jax import lax
from jax.experimental import pallas as pl
from jax.experimental.pallas import tpu as pltpu
from jax.sharding import PartitionSpec as P

D = 2048
HD = 128
TOPK = 10
F32 = jnp.float32
BF16 = jnp.bfloat16
HEAD = ("z2", "z1", "z0", "core")
SUB = ("y2", "y1", "y0")
EVERY = ("grp", "core", "y0", "z0", "y1", "z1", "y2", "z2")

VM = pl.BlockSpec(memory_space=pltpu.VMEM)
SM = pl.BlockSpec(memory_space=pltpu.SMEM)
HB = pl.BlockSpec(memory_space=pltpu.HBM)
KEEP = pl.BlockSpec(memory_space=pltpu.HBM)


class Fetched:
    def __init__(self, src, dst, sem):
        self.copy = pltpu.make_async_copy(src, dst, sem)
        self.copy.start()
        self.dst = dst
        self.done = False

    def get(self):
        if not self.done:
            self.copy.wait()
            self.done = True
        return self.dst


def call(body, outs, ins, operands, scratch=(), vmem=32 << 20):
    fetched = [i for i, spec in enumerate(ins) if spec is HB]
    buffers = [pltpu.VMEM(operands[i].shape, operands[i].dtype) for i in fetched]

    def kernel(*refs):
        refs = list(refs)
        if fetched:
            sems = refs.pop()
            dsts = refs[len(refs) - len(fetched) :]
            refs = refs[: len(refs) - len(fetched)]
            for j, i in enumerate(fetched):
                refs[i] = Fetched(refs[i], dsts[j], sems.at[j])
        body(*refs)

    operands = [
        pltpu.with_memory_space_constraint(o, pltpu.HBM) if ins[i] is HB or ins[i] is KEEP else o
        for i, o in enumerate(operands)
    ]
    extra = buffers + ([pltpu.SemaphoreType.DMA((len(fetched),))] if fetched else [])
    return pl.pallas_call(
        kernel,
        out_shape=outs,
        in_specs=ins,
        out_specs=jax.tree.map(lambda _: VM, outs),
        scratch_shapes=list(scratch) + extra,
        compiler_params=pltpu.CompilerParams(vmem_limit_bytes=vmem),
    )(*operands)


def split_hi(x):
    hi = x.astype(BF16).astype(F32)
    return hi, x - hi


def project_body(head_ref, x_in, gain_in, w_in, wab_in, *rest):
    held, out_ref, resid_ref, kept, sems = rest[:5], rest[5], rest[6], rest[7:12], rest[12]
    copies = [pltpu.make_async_copy(held[i], kept[i], sems.at[i]) for i in range(5)]
    for copy in copies:
        copy.start()
    x_ref = x_in.get()
    xf = x_ref[...].astype(F32)
    xg = (xf * gain_in.get()[...]).astype(BF16)
    head = head_ref[0]
    start = pl.multiple_of(lax.div(head, 2) * 16, 16)
    near = x_ref[pl.ds(start, 16), :].astype(F32)
    resid_ref[...] = jnp.where(lax.rem(head, 2) == 1, near[8:], near[:8])
    wab_ref = wab_in.get()
    xgf = xg.astype(F32)
    a = jnp.sum(xgf * wab_ref[0:1, :].astype(F32), axis=1, keepdims=True)
    b = jnp.sum(xgf * wab_ref[1:2, :].astype(F32), axis=1, keepdims=True)
    s = jnp.sum(xf * xf, axis=1, keepdims=True)
    lane = lax.broadcasted_iota(jnp.int32, (xf.shape[0], 128), 1)
    tail = jnp.zeros((xf.shape[0], 128), F32)
    at = 0
    for v in (a, b, s):
        hi, lo = split_hi(v)
        tail = jnp.where(lane == at, hi, tail)
        tail = jnp.where(lane == at + 1, lo, tail)
        at += 2
    out_ref[:, 640:] = tail.astype(BF16)
    proj = jnp.dot(xg, w_in.get()[...], preferred_element_type=F32)
    key_hi, key_lo = split_hi(proj[:, 128:256])
    out_ref[:, :128] = proj[:, :128].astype(BF16)
    out_ref[:, 128:256] = key_hi.astype(BF16)
    out_ref[:, 256:512] = proj[:, 256:].astype(BF16)
    out_ref[:, 512:640] = key_lo.astype(BF16)
    for copy in copies:
        copy.wait()


def silu(x):
    return x * jax.nn.sigmoid(x)


def recur_body(
    p_ref, alog_ref, bias_ref, sv_ref, ss_ref, gain_ref, gated_ref, keys_ref, delta_ref, sd_ref
):
    rows = 16
    t = p_ref[0].astype(F32)
    for i in range(1, 8):
        t = t + p_ref[i].astype(F32)
    tail = t[:, 640:]
    lane = lax.broadcasted_iota(jnp.int32, (rows, 128), 1)

    def column(i):
        return jnp.sum(
            jnp.where((lane == i) | (lane == i + 1), tail, 0.0), axis=1, keepdims=True
        )

    scale = lax.rsqrt(column(4) / D + 1e-05)
    proj = t[:, :512] * scale
    av = column(0) * scale
    bv = column(2) * scale
    query = silu(proj[:, :128])
    keys = silu(proj[:, 128:256] + t[:, 512:640] * scale)
    value = silu(proj[:, 256:384])
    zgate = proj[:, 384:512]
    query = (
        query
        * lax.rsqrt(jnp.sum(query * query, axis=-1, keepdims=True) + 1e-06)
        * (1.0 / 128.0**0.5)
    )
    keys = keys * lax.rsqrt(jnp.sum(keys * keys, axis=-1, keepdims=True) + 1e-06)
    beta = jax.nn.sigmoid(bv)
    rate = jnp.exp(jnp.zeros((1, 1), F32) + alog_ref[0])
    pre = av + bias_ref[0]
    soft = jnp.maximum(pre, 0.0) + jnp.log(1.0 + jnp.exp(-jnp.abs(pre)))
    decay = jnp.exp(-rate * soft)
    sd = ss_ref[...] * decay
    kd = (keys * sd).T
    qd = (query * sd).T
    mems = []
    cores = []
    for r in range(rows):
        v = sv_ref[r].astype(F32)
        mems.append(jnp.sum(v * kd[:, r : r + 1], axis=0, keepdims=True))
        cores.append(jnp.sum(v * qd[:, r : r + 1], axis=0, keepdims=True))
    memory = jnp.concatenate(mems, axis=0)
    core0 = jnp.concatenate(cores, axis=0)
    delta = (value - memory) * beta
    core = core0 + jnp.sum(query * keys, axis=-1, keepdims=True) * delta
    gated = (
        core
        * lax.rsqrt(jnp.mean(core * core, axis=-1, keepdims=True) + 1e-06)
        * gain_ref[...]
        * silu(zgate)
    )
    gated = gated.astype(BF16)
    for i in range(8):
        gated_ref[i] = gated
    keys_ref[...] = keys
    delta_ref[...] = delta
    sd_ref[...] = sd


def state_body(sv_ref, sd_ref, keys_ref, delta_ref, nv_ref, ns_ref):
    rows = 16
    sdt = sd_ref[...].T
    kt = keys_ref[...].T
    lane = lax.broadcasted_iota(jnp.int32, (128, rows), 1)
    peaks = jnp.zeros((128, rows), F32)
    for r in range(rows):
        s = sv_ref[r].astype(F32) * sdt[:, r : r + 1] + kt[:, r : r + 1] * delta_ref[r : r + 1, :]
        peak = jnp.max(jnp.abs(s), axis=1, keepdims=True) + 1e-06
        nv_ref[r] = (s / peak).astype(BF16)
        peaks = jnp.where(lane == r, peak, peaks)
    ns_ref[...] = peaks.T


def route_body(routes_in, scale_in, after_ref, mt_ref, w_ref):
    routes_ref, scale_ref = routes_in.get(), scale_in.get()
    n = 2048
    lane = lax.broadcasted_iota(jnp.int32, (8, n), 1)

    def bit(i):
        return (lane >> (i + 2)) & 1

    z = bit(0) * 4 + bit(2) * 2 + bit(4)
    expert = (((lane >> 9) * 8 + z) * 2 + bit(6)) * 4 + bit(1) * 2 + bit(3)
    slot_of = (lane >> 1) & 1
    half = lane % 2
    sends = jnp.zeros((8, n), F32)
    weight = jnp.zeros((8, n), F32)
    for k in range(TOPK):
        hit = routes_ref[:, k : k + 1] == expert
        sends = jnp.where(hit, 1.0, sends)
        weight = jnp.where(hit, scale_ref[:, k : k + 1].astype(F32) / 32.0, weight)
    row = lax.broadcasted_iota(jnp.int32, (8, n), 0)
    slot = jnp.zeros((8, n), F32)
    for r in range(7):
        slot = slot + jnp.where(row > r, sends[r : r + 1, :], 0.0)
    keep = (sends > 0.0) & (slot == slot_of.astype(F32))
    sel = jnp.where(keep, 1.0, 0.0)
    wsel = jnp.where(keep, weight, 0.0)
    first = half == 0
    selects = [jnp.where(first, sel, 0.0), jnp.where(first, 0.0, sel)]
    weights = [jnp.where(first, wsel, 0.0), jnp.where(first, 0.0, wsel)]
    mt_ref[...] = jnp.concatenate(selects, axis=0).T.astype(BF16)
    w_ref[...] = jnp.concatenate(weights, axis=0).astype(BF16)


def outproj_body(x_ref, w_ref, out_ref):
    out_ref[...] = jnp.dot(x_ref[...], w_ref[...], preferred_element_type=F32).astype(BF16)


def dispatch_body(attn_ref, resid_ref, mt_ref, hidden_ref, out_ref):
    attn = jnp.sum(attn_ref[...].astype(F32), axis=0)
    hidden = (resid_ref[...] + attn).astype(BF16)
    hidden_ref[...] = hidden
    hf = hidden.astype(F32)
    halves = jnp.concatenate([hf[:, :128], hf[:, 128:]], axis=0).astype(BF16)
    sent = jnp.dot(mt_ref[...], halves, preferred_element_type=F32)
    out_ref[...] = sent.reshape(512, 4, 128).astype(BF16)


def expert_body(x_ref, gain_ref, wgu_ref, wd_ref, out_ref, scr):
    scr[...] = x_ref[...].astype(F32).reshape(2048, 128)

    def rows_of(c, slot, z, half):
        at = (c & 1) * 32 + (z & 1) * 16 + (c >> 1 & 1) * 8 + (z >> 1 & 1) * 4
        at = at + (c >> 2) * 2 + (z >> 2)
        return pl.ds(at * 4 + slot * 2 + half, 8, stride=256)

    where = [(slot, z) for slot in range(2) for z in range(8)]
    sq = jnp.zeros((128, 128), F32)
    acc = jnp.zeros((128, 512), F32)
    for c in range(8):
        halves = [
            jnp.concatenate([scr[rows_of(c, slot, z, half), :] for slot, z in where], axis=0)
            for half in range(2)
        ]
        sq = sq + halves[0] * halves[0] + halves[1] * halves[1]
        xc = (jnp.concatenate(halves, axis=1) * gain_ref[c]).astype(BF16)
        acc = acc + jnp.dot(
            xc, wgu_ref[0, c * 256 : (c + 1) * 256, :], preferred_element_type=F32
        )
    acc = acc * lax.rsqrt(jnp.sum(sq, axis=1, keepdims=True) / D + 1e-05)
    act = (silu(acc[:, :256]) * acc[:, 256:]).astype(BF16)
    for c in range(8):
        o = jnp.dot(act, wd_ref[0, :, c * 256 : (c + 1) * 256], preferred_element_type=F32)
        for i, (slot, z) in enumerate(where):
            for half in range(2):
                scr[rows_of(c, slot, z, half), :] = o[
                    i * 8 : (i + 1) * 8, half * 128 : (half + 1) * 128
                ]
    out_ref[...] = scr[...].reshape(512, 4, 128).astype(BF16)


def combine_body(w_ref, x_ref, hidden_ref, out_ref):
    x = x_ref[...].astype(F32).reshape(2048, 128).astype(BF16)
    moe = jnp.dot(w_ref[...], x, preferred_element_type=F32)
    moe = jnp.concatenate([moe[:8], moe[8:]], axis=1)
    out_ref[...] = (hidden_ref[...].astype(F32) + moe).astype(BF16)


def shape(dims, dtype=BF16):
    return jax.ShapeDtypeStruct(dims, dtype)


def a2a(x, axes):
    return lax.all_to_all(x, axes, split_axis=0, concat_axis=0, tiled=True)


def local(
    inputs,
    in_gain,
    w_qkvz,
    w_ab,
    a_log,
    dt_bias,
    state_values,
    state_scales,
    norm_gain,
    w_out,
    post_gain,
    routes,
    route_scale,
    w_gate_up,
    w_down,
):
    head = lax.axis_index(HEAD).astype(jnp.int32).reshape(1)
    sv = state_values.reshape(16, 128, 128)
    ss = state_scales.reshape(16, 128)
    part, resid, sv, ss, ngain, w_out, pgain = call(
        project_body,
        (
            shape((128, 768)),
            shape((8, 256), F32),
            shape((16, 128, 128)),
            shape((16, 128), F32),
            shape((1, 128), F32),
            shape((128, 256)),
            shape((8, 1, 256), F32),
        ),
        [SM, HB, HB, HB, HB] + [KEEP] * 5,
        (
            head,
            inputs,
            in_gain.reshape(1, 256),
            w_qkvz,
            w_ab.T,
            sv,
            ss,
            norm_gain.reshape(1, 128),
            w_out,
            post_gain.reshape(8, 1, 256),
        ),
        [pltpu.SemaphoreType.DMA((5,))],
    )
    part = a2a(part.reshape(8, 16, 768), SUB)
    gated, keys, delta, sd = call(
        recur_body,
        (shape((8, 16, 128)), shape((16, 128), F32), shape((16, 128), F32), shape((16, 128), F32)),
        [VM, SM, SM, VM, VM, VM],
        (part, a_log, dt_bias, sv, ss, ngain),
    )
    mt, wsel = call(
        route_body,
        (shape((2048, 16)), shape((16, 2048))),
        [HB, HB, VM],
        (routes, route_scale, sd),
    )
    gathered = a2a(gated, SUB).reshape(128, 128)
    new_values, new_scales = call(
        state_body,
        (shape((16, 128, 128)), shape((16, 128), F32)),
        [VM] * 4,
        (sv, sd, keys, delta),
    )
    attn = call(outproj_body, shape((128, 256)), [VM] * 2, (gathered, w_out))
    attn = a2a(attn.reshape(16, 8, 256), HEAD)
    hidden, sent = call(
        dispatch_body,
        (shape((8, 256)), shape((512, 4, 128))),
        [VM] * 3,
        (attn, resid, mt),
    )
    received = a2a(sent, EVERY)
    result = call(
        expert_body,
        shape((512, 4, 128)),
        [VM] * 4,
        (received, pgain, w_gate_up, w_down),
        [pltpu.VMEM((2048, 128), F32)],
    )
    back = a2a(result, EVERY)
    out = call(combine_body, shape((8, 256)), [VM] * 3, (wsel, back, hidden))
    return (out, new_values.reshape(16, 1, 128, 128), new_scales.reshape(16, 1, 128))


def solution(mesh):
    names = ("grp",) + HEAD + SUB
    parts = (mesh.shape["grp"],) + (2,) * 7
    mesh = jax.sharding.Mesh(mesh.devices.reshape(parts), names)
    rows = ("grp",) + SUB
    placed = (
        P("grp", SUB),
        P(SUB),
        P(SUB, HEAD),
        P(SUB, HEAD),
        P(HEAD),
        P(HEAD),
        P(rows, HEAD, None, None),
        P(rows, HEAD, None),
        P(),
        P(HEAD, SUB),
        P(),
        P(("grp",) + HEAD, None),
        P(("grp",) + HEAD, None),
        P(names, None, None),
        P(names, None, None),
    )
    return jax.shard_map(
        local,
        mesh=mesh,
        in_specs=placed,
        out_specs=(P(("grp",) + HEAD, SUB), P(rows, HEAD, None, None), P(rows, HEAD, None)),
        check_vma=False,
    )
```

```python
import jax
import jax.numpy as jnp
from jax import lax
from jax.experimental import pallas as pl
from jax.experimental.pallas import tpu as pltpu
from jax.sharding import PartitionSpec as P

D = 2048
HD = 128
TOPK = 10
F32 = jnp.float32
BF16 = jnp.bfloat16

VM = pl.BlockSpec(memory_space=pltpu.VMEM)
SM = pl.BlockSpec(memory_space=pltpu.SMEM)
HB = pl.BlockSpec(memory_space=pltpu.HBM)
KEEP = pl.BlockSpec(memory_space=pltpu.HBM)


class Fetched:
    def __init__(self, src, dst, sem):
        self.copy = pltpu.make_async_copy(src, dst, sem)
        self.copy.start()
        self.dst = dst
        self.done = False

    def get(self):
        if not self.done:
            self.copy.wait()
            self.done = True
        return self.dst


def call(body, outs, ins, operands, scratch=(), vmem=32 << 20):
    fetched = [i for i, spec in enumerate(ins) if spec is HB]
    buffers = [pltpu.VMEM(operands[i].shape, operands[i].dtype) for i in fetched]

    def kernel(*refs):
        refs = list(refs)
        if fetched:
            sems = refs.pop()
            dsts = refs[len(refs) - len(fetched) :]
            refs = refs[: len(refs) - len(fetched)]
            for j, i in enumerate(fetched):
                refs[i] = Fetched(refs[i], dsts[j], sems.at[j])
        body(*refs)

    operands = [
        pltpu.with_memory_space_constraint(o, pltpu.HBM) if ins[i] is HB or ins[i] is KEEP else o
        for i, o in enumerate(operands)
    ]
    extra = buffers + ([pltpu.SemaphoreType.DMA((len(fetched),))] if fetched else [])
    return pl.pallas_call(
        kernel,
        out_shape=outs,
        in_specs=ins,
        out_specs=jax.tree.map(lambda _: VM, outs),
        scratch_shapes=list(scratch) + extra,
        compiler_params=pltpu.CompilerParams(vmem_limit_bytes=vmem),
    )(*operands)


def split_hi(x):
    hi = x.astype(BF16).astype(F32)
    return hi, x - hi


def project_body(head_ref, x_in, gain_in, w_in, wab_in, *rest):
    held, out_ref, resid_ref, kept, sems = rest[:5], rest[5], rest[6], rest[7:12], rest[12]
    copies = [pltpu.make_async_copy(held[i], kept[i], sems.at[i]) for i in range(5)]
    for copy in copies:
        copy.start()
    x_ref = x_in.get()
    xf = x_ref[...].astype(F32)
    xg = (xf * gain_in.get()[...]).astype(BF16)
    head = head_ref[0]
    start = pl.multiple_of(lax.div(head, 2) * 16, 16)
    near = x_ref[pl.ds(start, 16), :].astype(F32)
    resid_ref[...] = jnp.where(lax.rem(head, 2) == 1, near[8:], near[:8])
    wab_ref = wab_in.get()
    xgf = xg.astype(F32)
    a = jnp.sum(xgf * wab_ref[0:1, :].astype(F32), axis=1, keepdims=True)
    b = jnp.sum(xgf * wab_ref[1:2, :].astype(F32), axis=1, keepdims=True)
    s = jnp.sum(xf * xf, axis=1, keepdims=True)
    lane = lax.broadcasted_iota(jnp.int32, (xf.shape[0], 128), 1)
    tail = jnp.zeros((xf.shape[0], 128), F32)
    at = 0
    for v in (a, b, s):
        hi, lo = split_hi(v)
        tail = jnp.where(lane == at, hi, tail)
        tail = jnp.where(lane == at + 1, lo, tail)
        at += 2
    out_ref[:, 640:] = tail.astype(BF16)
    proj = jnp.dot(xg, w_in.get()[...], preferred_element_type=F32)
    key_hi, key_lo = split_hi(proj[:, 128:256])
    out_ref[:, :128] = proj[:, :128].astype(BF16)
    out_ref[:, 128:256] = key_hi.astype(BF16)
    out_ref[:, 256:512] = proj[:, 256:].astype(BF16)
    out_ref[:, 512:640] = key_lo.astype(BF16)
    for copy in copies:
        copy.wait()


def silu(x):
    return x * jax.nn.sigmoid(x)


def recur_body(
    p_ref, alog_ref, bias_ref, sv_ref, ss_ref, gain_ref, gated_ref, keys_ref, delta_ref, sd_ref
):
    rows = 16
    t = p_ref[0].astype(F32)
    for i in range(1, 8):
        t = t + p_ref[i].astype(F32)
    tail = t[:, 640:]
    lane = lax.broadcasted_iota(jnp.int32, (rows, 128), 1)

    def column(i):
        return jnp.sum(
            jnp.where((lane == i) | (lane == i + 1), tail, 0.0), axis=1, keepdims=True
        )

    scale = lax.rsqrt(column(4) / D + 1e-05)
    proj = t[:, :512] * scale
    av = column(0) * scale
    bv = column(2) * scale
    query = silu(proj[:, :128])
    keys = silu(proj[:, 128:256] + t[:, 512:640] * scale)
    value = silu(proj[:, 256:384])
    zgate = proj[:, 384:512]
    query = (
        query
        * lax.rsqrt(jnp.sum(query * query, axis=-1, keepdims=True) + 1e-06)
        * (1.0 / 128.0**0.5)
    )
    keys = keys * lax.rsqrt(jnp.sum(keys * keys, axis=-1, keepdims=True) + 1e-06)
    beta = jax.nn.sigmoid(bv)
    rate = jnp.exp(jnp.zeros((1, 1), F32) + alog_ref[0])
    pre = av + bias_ref[0]
    soft = jnp.maximum(pre, 0.0) + jnp.log(1.0 + jnp.exp(-jnp.abs(pre)))
    decay = jnp.exp(-rate * soft)
    sd = ss_ref[...] * decay
    kd = (keys * sd).T
    qd = (query * sd).T
    mems = []
    cores = []
    for r in range(rows):
        v = sv_ref[r].astype(F32)
        mems.append(jnp.sum(v * kd[:, r : r + 1], axis=0, keepdims=True))
        cores.append(jnp.sum(v * qd[:, r : r + 1], axis=0, keepdims=True))
    memory = jnp.concatenate(mems, axis=0)
    core0 = jnp.concatenate(cores, axis=0)
    delta = (value - memory) * beta
    core = core0 + jnp.sum(query * keys, axis=-1, keepdims=True) * delta
    gated = (
        core
        * lax.rsqrt(jnp.mean(core * core, axis=-1, keepdims=True) + 1e-06)
        * gain_ref[...]
        * silu(zgate)
    )
    gated = gated.astype(BF16)
    for i in range(8):
        gated_ref[i] = gated
    keys_ref[...] = keys
    delta_ref[...] = delta
    sd_ref[...] = sd


def state_body(sv_ref, sd_ref, keys_ref, delta_ref, nv_ref, ns_ref, done_ref):
    done_ref[...] = jnp.zeros((8, 128), F32)
    rows = 16
    sdt = sd_ref[...].T
    kt = keys_ref[...].T
    lane = lax.broadcasted_iota(jnp.int32, (128, rows), 1)
    peaks = jnp.zeros((128, rows), F32)
    for r in range(rows):
        s = sv_ref[r].astype(F32) * sdt[:, r : r + 1] + kt[:, r : r + 1] * delta_ref[r : r + 1, :]
        peak = jnp.max(jnp.abs(s), axis=1, keepdims=True) + 1e-06
        nv_ref[r] = (s * (1.0 / peak)).astype(BF16)
        peaks = jnp.where(lane == r, peak, peaks)
    ns_ref[...] = peaks.T


def route_body(routes_in, scale_in, mt_ref, w_ref):
    routes_ref, scale_ref = routes_in.get(), scale_in.get()
    n = 2048
    lane = lax.broadcasted_iota(jnp.int32, (8, n), 1)
    expert = lane // 8
    slot_of = lane // 2 % 2
    half = lane % 2
    sends = jnp.zeros((8, n), F32)
    weight = jnp.zeros((8, n), F32)
    for k in range(TOPK):
        hit = routes_ref[:, k : k + 1] == expert
        sends = jnp.where(hit, 1.0, sends)
        weight = jnp.where(hit, scale_ref[:, k : k + 1].astype(F32) / 32.0, weight)
    row = lax.broadcasted_iota(jnp.int32, (8, n), 0)
    slot = jnp.zeros((8, n), F32)
    for r in range(7):
        slot = slot + jnp.where(row > r, sends[r : r + 1, :], 0.0)
    keep = (sends > 0.0) & (slot == slot_of.astype(F32))
    sel = jnp.where(keep, 1.0, 0.0)
    wsel = jnp.where(keep, weight, 0.0)
    first = half == 0
    selects = [jnp.where(first, sel, 0.0), jnp.where(first, 0.0, sel)]
    weights = [jnp.where(first, wsel, 0.0), jnp.where(first, 0.0, wsel)]
    mt_ref[...] = jnp.concatenate(selects, axis=0).T.astype(BF16)
    w_ref[...] = jnp.concatenate(weights, axis=0).astype(BF16)


def outproj_body(x_ref, w_ref, out_ref):
    out_ref[...] = jnp.dot(x_ref[...], w_ref[...], preferred_element_type=F32).astype(BF16)


def dispatch_body(attn_ref, resid_ref, mt_ref, after_ref, hidden_ref, out_ref):
    attn = jnp.sum(attn_ref[...].astype(F32), axis=0)
    hidden = (resid_ref[...] + attn).astype(BF16)
    hidden_ref[...] = hidden
    hf = hidden.astype(F32)
    halves = jnp.concatenate([hf[:, :128], hf[:, 128:]], axis=0).astype(BF16)
    sent = jnp.dot(mt_ref[...], halves, preferred_element_type=F32)
    out_ref[...] = sent.astype(BF16)


def expert_body(x_ref, gain_ref, wgu_ref, wd_ref, out_ref, scr):
    scr[...] = x_ref[...].astype(F32)

    def rows_of(c, slot, half):
        return pl.ds(c * 4 + slot * 2 + half, 64, stride=32)

    sq = jnp.zeros((128, 128), F32)
    acc = jnp.zeros((128, 512), F32)
    for c in range(8):
        halves = [
            jnp.concatenate([scr[rows_of(c, slot, half), :] for slot in range(2)], axis=0)
            for half in range(2)
        ]
        sq = sq + halves[0] * halves[0] + halves[1] * halves[1]
        xc = (jnp.concatenate(halves, axis=1) * gain_ref[c]).astype(BF16)
        acc = acc + jnp.dot(
            xc, wgu_ref[0, c * 256 : (c + 1) * 256, :], preferred_element_type=F32
        )
    acc = acc * lax.rsqrt(jnp.sum(sq, axis=1, keepdims=True) / D + 1e-05)
    act = (silu(acc[:, :256]) * acc[:, 256:]).astype(BF16)
    for c in range(8):
        o = jnp.dot(act, wd_ref[0, :, c * 256 : (c + 1) * 256], preferred_element_type=F32)
        for slot in range(2):
            for half in range(2):
                scr[rows_of(c, slot, half), :] = o[
                    slot * 64 : (slot + 1) * 64, half * 128 : (half + 1) * 128
                ]
    out_ref[...] = scr[...].astype(BF16)


def combine_body(w_ref, x_ref, hidden_ref, out_ref):
    moe = jnp.dot(w_ref[...], x_ref[...], preferred_element_type=F32)
    moe = jnp.concatenate([moe[:8], moe[8:]], axis=1)
    out_ref[...] = (hidden_ref[...].astype(F32) + moe).astype(BF16)


def shape(dims, dtype=BF16):
    return jax.ShapeDtypeStruct(dims, dtype)


def a2a(x, axes):
    return lax.all_to_all(x, axes, split_axis=0, concat_axis=0, tiled=True)


def local(
    inputs,
    in_gain,
    w_qkvz,
    w_ab,
    a_log,
    dt_bias,
    state_values,
    state_scales,
    norm_gain,
    w_out,
    post_gain,
    routes,
    route_scale,
    w_gate_up,
    w_down,
):
    head = lax.axis_index("head").astype(jnp.int32).reshape(1)
    sv = state_values.reshape(16, 128, 128)
    ss = state_scales.reshape(16, 128)
    part, resid, sv, ss, ngain, w_out, pgain = call(
        project_body,
        (
            shape((128, 768)),
            shape((8, 256), F32),
            shape((16, 128, 128)),
            shape((16, 128), F32),
            shape((1, 128), F32),
            shape((128, 256)),
            shape((8, 1, 256), F32),
        ),
        [SM, HB, HB, HB, HB] + [KEEP] * 5,
        (
            head,
            inputs,
            in_gain.reshape(1, 256),
            w_qkvz,
            w_ab.T,
            sv,
            ss,
            norm_gain.reshape(1, 128),
            w_out,
            post_gain.reshape(8, 1, 256),
        ),
        [pltpu.SemaphoreType.DMA((5,))],
    )
    part = a2a(part.reshape(8, 16, 768), "sub")
    mt, wsel = call(
        route_body,
        (shape((2048, 16)), shape((16, 2048))),
        [HB, HB],
        (routes, route_scale),
    )
    gated, keys, delta, sd = call(
        recur_body,
        (shape((8, 16, 128)), shape((16, 128), F32), shape((16, 128), F32), shape((16, 128), F32)),
        [VM, SM, SM, VM, VM, VM],
        (part, a_log, dt_bias, sv, ss, ngain),
    )
    gathered = a2a(gated, "sub").reshape(128, 128)
    new_values, new_scales, done = call(
        state_body,
        (shape((16, 128, 128)), shape((16, 128), F32), shape((8, 128), F32)),
        [VM] * 4,
        (sv, sd, keys, delta),
    )
    attn = call(outproj_body, shape((128, 256)), [VM] * 2, (gathered, w_out))
    attn = a2a(attn.reshape(16, 8, 256), "head")
    hidden, sent = call(
        dispatch_body,
        (shape((8, 256)), shape((2048, 128))),
        [VM] * 4,
        (attn, resid, mt, done),
    )
    every = ("grp", "head", "sub")
    received = a2a(sent.reshape(512, 4, 128), every).reshape(2048, 128)
    result = call(
        expert_body,
        shape((2048, 128)),
        [VM] * 4,
        (received, pgain, w_gate_up, w_down),
        [pltpu.VMEM((2048, 128), F32)],
    )
    back = a2a(result.reshape(512, 4, 128), every).reshape(2048, 128)
    out = call(combine_body, shape((8, 256)), [VM] * 3, (wsel, back, hidden))
    return (out, new_values.reshape(16, 1, 128, 128), new_scales.reshape(16, 1, 128))


def solution(mesh):
    placed = (
        P("grp", "sub"),
        P("sub"),
        P("sub", "head"),
        P("sub", "head"),
        P("head"),
        P("head"),
        P(("grp", "sub"), "head", None, None),
        P(("grp", "sub"), "head", None),
        P(),
        P("head", "sub"),
        P(),
        P(("grp", "head"), None),
        P(("grp", "head"), None),
        P(("grp", "head", "sub"), None, None),
        P(("grp", "head", "sub"), None, None),
    )
    return jax.shard_map(
        local,
        mesh=mesh,
        in_specs=placed,
        out_specs=(
            P(("grp", "head"), "sub"),
            P(("grp", "sub"), "head", None, None),
            P(("grp", "sub"), "head", None),
        ),
        check_vma=False,
    )
```

```python
import jax
import jax.numpy as jnp
from jax import lax
from jax.experimental import pallas as pl
from jax.experimental.pallas import tpu as pltpu
from jax.sharding import PartitionSpec as P

D = 2048
HD = 128
TOPK = 10
F32 = jnp.float32
BF16 = jnp.bfloat16
SUB = ("quad", "side")

VM = pl.BlockSpec(memory_space=pltpu.VMEM)
SM = pl.BlockSpec(memory_space=pltpu.SMEM)
HB = pl.BlockSpec(memory_space=pltpu.HBM)
KEEP = pl.BlockSpec(memory_space=pltpu.HBM)


class Fetched:
    def __init__(self, src, dst, sem):
        self.copy = pltpu.make_async_copy(src, dst, sem)
        self.copy.start()
        self.dst = dst
        self.done = False

    def get(self):
        if not self.done:
            self.copy.wait()
            self.done = True
        return self.dst


def call(body, outs, ins, operands, scratch=(), vmem=32 << 20):
    fetched = [i for i, spec in enumerate(ins) if spec is HB]
    buffers = [pltpu.VMEM(operands[i].shape, operands[i].dtype) for i in fetched]

    def kernel(*refs):
        refs = list(refs)
        if fetched:
            sems = refs.pop()
            dsts = refs[len(refs) - len(fetched) :]
            refs = refs[: len(refs) - len(fetched)]
            for j, i in enumerate(fetched):
                refs[i] = Fetched(refs[i], dsts[j], sems.at[j])
        body(*refs)

    operands = [
        pltpu.with_memory_space_constraint(o, pltpu.HBM) if ins[i] is HB or ins[i] is KEEP else o
        for i, o in enumerate(operands)
    ]
    extra = buffers + ([pltpu.SemaphoreType.DMA((len(fetched),))] if fetched else [])
    return pl.pallas_call(
        kernel,
        out_shape=outs,
        in_specs=ins,
        out_specs=jax.tree.map(lambda _: VM, outs),
        scratch_shapes=list(scratch) + extra,
        compiler_params=pltpu.CompilerParams(vmem_limit_bytes=vmem),
    )(*operands)


def split_hi(x):
    hi = x.astype(BF16).astype(F32)
    return hi, x - hi


def project_body(head_ref, x_in, gain_in, w_in, wab_in, *rest):
    held, out_ref, resid_ref, kept, sems = rest[:5], rest[5], rest[6], rest[7:12], rest[12]
    copies = [pltpu.make_async_copy(held[i], kept[i], sems.at[i]) for i in range(5)]
    for copy in copies:
        copy.start()
    x_ref = x_in.get()
    xf = x_ref[...].astype(F32)
    xg = (xf * gain_in.get()[...]).astype(BF16)
    head = head_ref[0]
    start = pl.multiple_of(lax.div(head, 2) * 16, 16)
    near = x_ref[pl.ds(start, 16), :].astype(F32)
    resid_ref[...] = jnp.where(lax.rem(head, 2) == 1, near[8:], near[:8])
    wab_ref = wab_in.get()
    xgf = xg.astype(F32)
    a = jnp.sum(xgf * wab_ref[0:1, :].astype(F32), axis=1, keepdims=True)
    b = jnp.sum(xgf * wab_ref[1:2, :].astype(F32), axis=1, keepdims=True)
    s = jnp.sum(xf * xf, axis=1, keepdims=True)
    lane = lax.broadcasted_iota(jnp.int32, (xf.shape[0], 128), 1)
    tail = jnp.zeros((xf.shape[0], 128), F32)
    at = 0
    for v in (a, b, s):
        hi, lo = split_hi(v)
        tail = jnp.where(lane == at, hi, tail)
        tail = jnp.where(lane == at + 1, lo, tail)
        at += 2
    out_ref[:, 640:] = tail.astype(BF16)
    proj = jnp.dot(xg, w_in.get()[...], preferred_element_type=F32)
    key_hi, key_lo = split_hi(proj[:, 128:256])
    out_ref[:, :128] = proj[:, :128].astype(BF16)
    out_ref[:, 128:256] = key_hi.astype(BF16)
    out_ref[:, 256:512] = proj[:, 256:].astype(BF16)
    out_ref[:, 512:640] = key_lo.astype(BF16)
    for copy in copies:
        copy.wait()


def silu(x):
    return x * jax.nn.sigmoid(x)


def recur_body(
    p_ref, alog_ref, bias_ref, sv_ref, ss_ref, gain_ref, gated_ref, keys_ref, delta_ref, sd_ref
):
    rows = 16
    t = p_ref[0].astype(F32)
    for i in range(1, 8):
        t = t + p_ref[i].astype(F32)
    tail = t[:, 640:]
    lane = lax.broadcasted_iota(jnp.int32, (rows, 128), 1)

    def column(i):
        return jnp.sum(
            jnp.where((lane == i) | (lane == i + 1), tail, 0.0), axis=1, keepdims=True
        )

    scale = lax.rsqrt(column(4) / D + 1e-05)
    proj = t[:, :512] * scale
    av = column(0) * scale
    bv = column(2) * scale
    query = silu(proj[:, :128])
    keys = silu(proj[:, 128:256] + t[:, 512:640] * scale)
    value = silu(proj[:, 256:384])
    zgate = proj[:, 384:512]
    query = (
        query
        * lax.rsqrt(jnp.sum(query * query, axis=-1, keepdims=True) + 1e-06)
        * (1.0 / 128.0**0.5)
    )
    keys = keys * lax.rsqrt(jnp.sum(keys * keys, axis=-1, keepdims=True) + 1e-06)
    beta = jax.nn.sigmoid(bv)
    rate = jnp.exp(jnp.zeros((1, 1), F32) + alog_ref[0])
    pre = av + bias_ref[0]
    soft = jnp.maximum(pre, 0.0) + jnp.log(1.0 + jnp.exp(-jnp.abs(pre)))
    decay = jnp.exp(-rate * soft)
    sd = ss_ref[...] * decay
    kd = (keys * sd).T
    qd = (query * sd).T
    mems = []
    cores = []
    for r in range(rows):
        v = sv_ref[r].astype(F32)
        mems.append(jnp.sum(v * kd[:, r : r + 1], axis=0, keepdims=True))
        cores.append(jnp.sum(v * qd[:, r : r + 1], axis=0, keepdims=True))
    memory = jnp.concatenate(mems, axis=0)
    core0 = jnp.concatenate(cores, axis=0)
    delta = (value - memory) * beta
    core = core0 + jnp.sum(query * keys, axis=-1, keepdims=True) * delta
    gated = (
        core
        * lax.rsqrt(jnp.mean(core * core, axis=-1, keepdims=True) + 1e-06)
        * gain_ref[...]
        * silu(zgate)
    )
    gated = gated.astype(BF16)
    for i in range(8):
        gated_ref[i] = gated
    keys_ref[...] = keys
    delta_ref[...] = delta
    sd_ref[...] = sd


def state_body(sv_ref, sd_ref, keys_ref, delta_ref, nv_ref, ns_ref):
    rows = 16
    sdt = sd_ref[...].T
    kt = keys_ref[...].T
    lane = lax.broadcasted_iota(jnp.int32, (128, rows), 1)
    peaks = jnp.zeros((128, rows), F32)
    for r in range(rows):
        s = sv_ref[r].astype(F32) * sdt[:, r : r + 1] + kt[:, r : r + 1] * delta_ref[r : r + 1, :]
        peak = jnp.max(jnp.abs(s), axis=1, keepdims=True) + 1e-06
        nv_ref[r] = (s * (1.0 / peak)).astype(BF16)
        peaks = jnp.where(lane == r, peak, peaks)
    ns_ref[...] = peaks.T


def route_body(routes_in, scale_in, mt_ref, w_ref):
    routes_ref, scale_ref = routes_in.get(), scale_in.get()
    n = 1024
    lane = lax.broadcasted_iota(jnp.int32, (8, n), 1)
    expert = lane // 4
    slot_of = lane // 2 % 2
    half = lane % 2
    sends = jnp.zeros((8, n), F32)
    weight = jnp.zeros((8, n), F32)
    for k in range(TOPK):
        hit = routes_ref[:, k : k + 1] == expert
        sends = jnp.where(hit, 1.0, sends)
        weight = jnp.where(hit, scale_ref[:, k : k + 1].astype(F32) / 32.0, weight)
    row = lax.broadcasted_iota(jnp.int32, (8, n), 0)
    slot = jnp.zeros((8, n), F32)
    for r in range(7):
        slot = slot + jnp.where(row > r, sends[r : r + 1, :], 0.0)
    keep = (sends > 0.0) & (slot == slot_of.astype(F32))
    sel = jnp.where(keep, 1.0, 0.0)
    wsel = jnp.where(keep, weight, 0.0)
    first = half == 0
    selects = [jnp.where(first, sel, 0.0), jnp.where(first, 0.0, sel)]
    weights = [jnp.where(first, wsel, 0.0), jnp.where(first, 0.0, wsel)]
    mt_ref[...] = jnp.concatenate(selects, axis=0).T.astype(BF16)
    w_ref[...] = jnp.concatenate(weights, axis=0).astype(BF16)


def outproj_body(x_ref, w_ref, out_ref):
    out_ref[...] = jnp.dot(x_ref[...], w_ref[...], preferred_element_type=F32).astype(BF16)


def dispatch_body(attn_ref, resid_ref, mt_ref, hidden_ref, out_ref):
    attn = jnp.sum(attn_ref[...].astype(F32), axis=0)
    hidden = (resid_ref[...] + attn).astype(BF16)
    hidden_ref[...] = hidden
    hf = hidden.astype(F32)
    halves = jnp.concatenate([hf[:, :128], hf[:, 128:]], axis=0).astype(BF16)
    sent = jnp.dot(mt_ref[...], halves, preferred_element_type=F32)
    out_ref[...] = sent.astype(BF16)


def expert_body(x_ref, gain_ref, wgu_ref, wd_ref, wgu2_ref, wd2_ref, out_ref, scr):
    scr[...] = x_ref[...].astype(F32)

    def rows_of(c, half):
        return pl.ds(c * 2 + half, 64, stride=16)

    sq = jnp.zeros((64, 128), F32)
    acc = jnp.zeros((64, 512), F32)
    acc2 = jnp.zeros((64, 512), F32)
    for c in range(8):
        halves = [scr[rows_of(c, half), :] for half in range(2)]
        sq = sq + halves[0] * halves[0] + halves[1] * halves[1]
        xc = (jnp.concatenate(halves, axis=1) * gain_ref[c]).astype(BF16)
        part = slice(c * 256, (c + 1) * 256)
        acc = acc + jnp.dot(xc, wgu_ref[0, part, :], preferred_element_type=F32)
        acc2 = acc2 + jnp.dot(xc, wgu2_ref[0, part, :], preferred_element_type=F32)
    rs = lax.rsqrt(jnp.sum(sq, axis=1, keepdims=True) / D + 1e-05)
    acc = acc * rs
    acc2 = acc2 * rs
    act = (silu(acc[:, :256]) * acc[:, 256:]).astype(BF16)
    act2 = (silu(acc2[:, :256]) * acc2[:, 256:]).astype(BF16)
    for c in range(8):
        part = slice(c * 256, (c + 1) * 256)
        o = jnp.dot(act, wd_ref[0, :, part], preferred_element_type=F32)
        o = o + jnp.dot(act2, wd2_ref[0, :, part], preferred_element_type=F32)
        for half in range(2):
            scr[rows_of(c, half), :] = o[:, half * 128 : (half + 1) * 128]
    out_ref[...] = scr[...].astype(BF16)


def combine_body(w_ref, x_ref, hidden_ref, out_ref):
    moe = jnp.dot(w_ref[...], x_ref[...], preferred_element_type=F32)
    moe = jnp.concatenate([moe[:8], moe[8:]], axis=1)
    out_ref[...] = (hidden_ref[...].astype(F32) + moe).astype(BF16)


def shape(dims, dtype=BF16):
    return jax.ShapeDtypeStruct(dims, dtype)


def a2a(x, axes):
    return lax.all_to_all(x, axes, split_axis=0, concat_axis=0, tiled=True)


def local(
    inputs,
    in_gain,
    w_qkvz,
    w_ab,
    a_log,
    dt_bias,
    state_values,
    state_scales,
    norm_gain,
    w_out,
    post_gain,
    routes,
    route_scale,
    w_gate_up,
    w_down,
):
    head = lax.axis_index("head").astype(jnp.int32).reshape(1)
    swap = [(0, 1), (1, 0)]
    w_gate_up2 = lax.ppermute(w_gate_up, "side", swap)
    w_down2 = lax.ppermute(w_down, "side", swap)
    sv = state_values.reshape(16, 128, 128)
    ss = state_scales.reshape(16, 128)
    part, resid, sv, ss, ngain, w_out, pgain = call(
        project_body,
        (
            shape((128, 768)),
            shape((8, 256), F32),
            shape((16, 128, 128)),
            shape((16, 128), F32),
            shape((1, 128), F32),
            shape((128, 256)),
            shape((8, 1, 256), F32),
        ),
        [SM, HB, HB, HB, HB] + [KEEP] * 5,
        (
            head,
            inputs,
            in_gain.reshape(1, 256),
            w_qkvz,
            w_ab.T,
            sv,
            ss,
            norm_gain.reshape(1, 128),
            w_out,
            post_gain.reshape(8, 1, 256),
        ),
        [pltpu.SemaphoreType.DMA((5,))],
    )
    part = a2a(part.reshape(8, 16, 768), SUB)
    mt, wsel = call(
        route_body,
        (shape((1024, 16)), shape((16, 1024))),
        [HB, HB],
        (routes, route_scale),
    )
    gated, keys, delta, sd = call(
        recur_body,
        (shape((8, 16, 128)), shape((16, 128), F32), shape((16, 128), F32), shape((16, 128), F32)),
        [VM, SM, SM, VM, VM, VM],
        (part, a_log, dt_bias, sv, ss, ngain),
    )
    gathered = a2a(gated, SUB).reshape(128, 128)
    new_values, new_scales = call(
        state_body,
        (shape((16, 128, 128)), shape((16, 128), F32)),
        [VM] * 4,
        (sv, sd, keys, delta),
    )
    attn = call(outproj_body, shape((128, 256)), [VM] * 2, (gathered, w_out))
    attn = a2a(attn.reshape(16, 8, 256), "head")
    hidden, sent = call(
        dispatch_body,
        (shape((8, 256)), shape((1024, 128))),
        [VM] * 3,
        (attn, resid, mt),
    )
    every = ("grp", "head") + SUB
    received = a2a(sent.reshape(512, 2, 128), every).reshape(1024, 128)
    result = call(
        expert_body,
        shape((1024, 128)),
        [VM] * 6,
        (received, pgain, w_gate_up, w_down, w_gate_up2, w_down2),
        [pltpu.VMEM((1024, 128), F32)],
    )
    back = a2a(result.reshape(512, 2, 128), every).reshape(1024, 128)
    out = call(combine_body, shape((8, 256)), [VM] * 3, (wsel, back, hidden))
    return (out, new_values.reshape(16, 1, 128, 128), new_scales.reshape(16, 1, 128))


def solution(mesh):
    shape4 = (mesh.shape["grp"], mesh.shape["head"], mesh.shape["sub"] // 2, 2)
    mesh = jax.sharding.Mesh(mesh.devices.reshape(shape4), ("grp", "head") + SUB)
    placed = (
        P("grp", SUB),
        P(SUB),
        P(SUB, "head"),
        P(SUB, "head"),
        P("head"),
        P("head"),
        P(("grp",) + SUB, "head", None, None),
        P(("grp",) + SUB, "head", None),
        P(),
        P("head", SUB),
        P(),
        P(("grp", "head"), None),
        P(("grp", "head"), None),
        P(("grp", "head") + SUB, None, None),
        P(("grp", "head") + SUB, None, None),
    )
    return jax.shard_map(
        local,
        mesh=mesh,
        in_specs=placed,
        out_specs=(
            P(("grp", "head"), SUB),
            P(("grp",) + SUB, "head", None, None),
            P(("grp",) + SUB, "head", None),
        ),
        check_vma=False,
    )
```
